512 devices in a mesh: dp: 128 (over z, x, y_hi, core), layer: 4 (over y_lo).
Axes of the slice: x: 4, y: 8 (y_hi: 2, y_lo: 4; y = y_hi * 4 + y_lo), z: 8, core: 2. Of those that a mesh axis runs over, the one named last changes fastest.
Arguments:
- activations: bfloat16 [4, 16384, 9728], P('layer', 'dp'), may hold values from -0.796875 to 1.1953125
- out_grads: bfloat16 [4, 16384, 3584], P('layer', 'dp'), may hold values from -0.796875 to 1.1953125
- in_basis: bfloat16 [4, 9728, 64], P('layer', 'dp'), may hold values from -0.0625 to 0.0625
- out_basis: bfloat16 [4, 3584, 64], P('layer', 'dp'), may hold values from -0.09375 to 0.09375
- queries: bfloat16 [4, 64, 4096], P('layer'), may hold values from -6 to 6
- pair_lengths: int32 [128, 4], P('dp'), may hold values from 1 to 32, 96 in all within a row
- query_index: int32 [512, 8], P('dp'), may hold values from 0 to 63
Outputs:
- sketches: bfloat16 [4, 512, 4096], P('layer', 'dp')
- scores: float32 [512, 8], P('dp')
The draws below stay inside these ranges and needn't reach their ends.
Inputs may be any that keep to these rules, and one draw needn't show every extreme that they name: `pair_lengths`: the lengths in one row sum to 96, and one of them is 32.
All inputs are finite; a program needn't handle non-finite values.
Results may differ from the reference program's by a relative error of at most 0.0062.
Values may be sent and summed in bfloat16 or wider, within the bound.
A program may use at most 64 MiB of HBM per device.

```python
import math
import jax
import jax.numpy as jnp
import numpy as np

D = 3584
FFW = 9728
KIN = 64
KOUT = 64
PAIRS_DEV = 4
PAIR_TOK = 32
NQ = 64
QSEL = 8
LAYERS = 4
PAIRS = 512
TOKENS = 16384
N_DP = 128


def plant(result, stream_key, least, top_value):
    extent = result.shape
    spot = [jax.random.randint(jax.random.fold_in(stream_key, axis), (), 0, extent[axis]) for axis in range(len(extent))]
    result = result.at[tuple(spot)].set(least)
    longest = extent.index(max(extent))
    spot[longest] = (spot[longest] + 1) % extent[longest]
    return result.at[tuple(spot)].set(top_value)


def shard_levels(stream_key, shape, split, low, high):
    gain = 1.0
    for dim, parts in split:
        heights = jax.random.uniform(jax.random.fold_in(jax.random.fold_in(stream_key, 6), dim), (parts,), jnp.float32, low / len(split), high / len(split))
        gain = gain * jnp.repeat(jnp.exp(heights), shape[dim] // parts).reshape((-1,) + (1,) * (len(shape) - 1 - dim))
    return gain


def profile(number_of, total, most, slope):
    weights = [(1 << 20) // math.isqrt(grade ** slope) + 1 for grade in range(2, number_of + 1)]
    rest, holding = total - most - (number_of - 1), [1] * (number_of - 1)
    while rest > 0:
        candidates = [i for i in range(number_of - 1) if holding[i] < most]
        whole, budget = sum([weights[i] for i in candidates]), rest
        for i in candidates:
            addition = min(most - holding[i], max(1, budget * weights[i] // whole), rest)
            holding[i] = holding[i] + addition
            rest = rest - addition
    return np.array([most] + holding)


def ragged(rng, number_of, total, reach, skew):
    if number_of == 2:
        one = jax.random.randint(rng, (), max(1, total - reach), min(reach, total - 1) + 1)
        return jnp.stack([one, total - one])
    tallies = jnp.asarray(profile(number_of, total, reach, skew), jnp.int32)
    couples = (number_of - 1) // 2
    source_of, sink = tallies[1:1 + 2 * couples:2], tallies[2:2 + 2 * couples:2]
    slack = jnp.minimum(source_of - 1, reach - sink)
    shifted = jax.random.randint(jax.random.fold_in(rng, 1), (couples,), 0, 1 << 20) % (slack + 1)
    tallies = tallies.at[1:1 + 2 * couples:2].set(source_of - shifted).at[2:2 + 2 * couples:2].set(sink + shifted)
    return tallies[jax.random.permutation(jax.random.fold_in(rng, 2), number_of)]


def noise(rng, dims, scale, limit, shards=(), kind=jnp.bfloat16):
    entries = scale * jax.random.normal(rng, dims, jnp.float32)
    if shards:
        entries = entries * shard_levels(rng, dims, shards, -0.22, 0.18)
    return jnp.clip(entries, -limit, limit).astype(kind)


def setup_inputs(seed: int = 0) -> dict:
    keys = jax.random.split(jax.random.key(seed), 8)
    activations = jnp.clip(-0.796875 + 1.9921875 * jax.random.uniform(keys[0], (LAYERS, TOKENS, FFW), jnp.float32) ** shard_levels(keys[0], (LAYERS, TOKENS, FFW), ((0, 4), (1, 128)), -0.2, 0.2), -0.796875, 1.1953125).astype(jnp.bfloat16)
    out_grads = jnp.clip(-0.796875 + 1.9921875 * jax.random.uniform(keys[1], (LAYERS, TOKENS, D), jnp.float32) ** shard_levels(keys[1], (LAYERS, TOKENS, D), ((0, 4), (1, 128)), -0.2, 0.2), -0.796875, 1.1953125).astype(jnp.bfloat16)
    in_basis = noise(keys[2], (LAYERS, FFW, KIN), FFW ** -0.5, 0.0625, ((0, 4), (1, 128)))
    out_basis = noise(keys[3], (LAYERS, D, KOUT), D ** -0.5, 0.09375, ((0, 4), (1, 128)))
    queries = noise(keys[4], (LAYERS, NQ, KOUT * KIN), 1.0, 6.0, ((0, 4),))
    pair_lengths = jax.vmap(lambda own: ragged(own, PAIRS_DEV, (PAIRS_DEV - 1) * PAIR_TOK, PAIR_TOK, 0))(jax.random.split(keys[5], N_DP)).reshape((N_DP, PAIRS_DEV)).astype(jnp.int32)
    query_index = plant(jax.random.randint(keys[6], (PAIRS, QSEL), 0, NQ), jax.random.fold_in(keys[6], 1), 0, NQ - 1).astype(jnp.int32)
    return {"activations": activations, "out_grads": out_grads, "in_basis": in_basis, "out_basis": out_basis, "queries": queries, "pair_lengths": pair_lengths, "query_index": query_index}


damp_ratio = 0.5

def reference(activations, out_grads, in_basis, out_basis, queries, pair_lengths, query_index):
    lengths_flat = pair_lengths.reshape(PAIRS)
    positions = jnp.arange(PAIR_TOK, dtype=jnp.int32)
    token_mask = (positions[None, :] < lengths_flat[:, None]).astype(jnp.float32).reshape(TOKENS, 1)
    kernel = jnp.zeros((PAIRS, PAIRS), jnp.float32)
    inner = jnp.zeros((PAIRS, NQ), jnp.float32)
    sketch_list = []
    for layer_idx in range(LAYERS):
        right_proj = jnp.dot(activations[layer_idx].astype(jnp.float32), in_basis[layer_idx].astype(jnp.float32), preferred_element_type=jnp.float32).astype(jnp.bfloat16)
        left_proj = (token_mask * jnp.dot(out_grads[layer_idx].astype(jnp.float32), out_basis[layer_idx].astype(jnp.float32), preferred_element_type=jnp.float32)).astype(jnp.bfloat16)
        left_pairs = left_proj.reshape(PAIRS, PAIR_TOK, KOUT).astype(jnp.float32)
        right_pairs = right_proj.reshape(PAIRS, PAIR_TOK, KIN).astype(jnp.float32)
        sketch = jnp.einsum('ptk,ptj->pkj', left_pairs, right_pairs).reshape(PAIRS, KOUT * KIN).astype(jnp.bfloat16)
        sketch_list.append(sketch)
        kernel = kernel + jnp.dot(sketch.astype(jnp.float32), sketch.T.astype(jnp.float32), preferred_element_type=jnp.float32)
        inner = inner + jnp.dot(sketch.astype(jnp.float32), queries[layer_idx].T.astype(jnp.float32), preferred_element_type=jnp.float32)
    mean_diag = jnp.trace(kernel) / PAIRS
    damping = damp_ratio * mean_diag
    factor = jnp.linalg.cholesky(kernel + damping * jnp.eye(PAIRS, dtype=jnp.float32))
    solved = jax.scipy.linalg.cho_solve((factor, True), inner)
    scores = jnp.sqrt(mean_diag) * jnp.take_along_axis(solved, query_index, axis=1)
    return (jnp.stack(sketch_list, 0), scores)
```

```python
import jax
import jax.numpy as jnp
from jax import lax
from jax.experimental import pallas as pl
from jax.experimental.pallas import tpu as pltpu
from jax.sharding import PartitionSpec as P

MESH = pl.DeviceIdType.MESH
damp_ratio = 0.5
F32 = jnp.float32
BF16 = jnp.bfloat16
NT = (((1,), (1,)), ((), ()))
SEMS = 128


def iota(shape, dim):
    return lax.broadcasted_iota(jnp.int32, shape, dim)


def onehot(cond):
    return jnp.where(cond, 1.0, 0.0).astype(BF16)


def pieces(v):
    hi = v.astype(BF16)
    rest = v - hi.astype(F32)
    mid = rest.astype(BF16)
    return hi, mid, (rest - mid.astype(F32)).astype(BF16)


def dot(a, b):
    return jnp.dot(a, b, preferred_element_type=F32)


def dot_nt(a, b):
    return lax.dot_general(a, b, NT, preferred_element_type=F32)


def front(act, grd, wblk, qblk, lens, sk, kin, av, gv, xs, wg, srow, scol, lx, kb, perm, acc, in_sem, ssem, rsem):
    me = lax.axis_index("dp")
    ly = lax.axis_index("layer")
    c = me % 2
    h = (me // 2) % 2
    x = (me // 4) % 4
    z = me // 16
    b = me % 16

    def at(zz, xx, hh, cc):
        return ((zz * 4 + xx) * 2 + hh) * 2 + cc

    h_peer = at(z, x, 1 - h, c)
    c_peer = at(z, x, h, 1 - c)
    x_peers = [at(z, (x + d) % 4, h, c) for d in range(1, 4)]
    z_peers = [at((z + d) % 8, x, h, c) for d in range(1, 8)]

    load_a = pltpu.make_async_copy(act, av, in_sem.at[0])
    load_g = pltpu.make_async_copy(grd, gv, in_sem.at[1])
    load_a.start()
    load_g.start()

    barrier = pltpu.get_barrier_semaphore()
    for peer in [h_peer, c_peer] + x_peers + z_peers:
        pl.semaphore_signal(barrier, inc=1, device_id={"dp": peer}, device_id_type=MESH)
    for d in range(1, 4):
        pl.semaphore_signal(barrier, inc=1, device_id={"layer": (ly + d) % 4}, device_id_type=MESH)

    used = [0]
    sent = []

    def take():
        used[0] += 1
        return used[0] - 1

    def send(src, dst, sem, device):
        copy = pltpu.make_async_remote_copy(
            src_ref=src, dst_ref=dst, send_sem=ssem.at[sem], recv_sem=rsem.at[sem], device_id=device, device_id_type=MESH
        )
        copy.start()
        sent.append(copy)

    def arrived(slot, sem):
        pltpu.make_async_remote_copy(
            src_ref=slot, dst_ref=slot, send_sem=ssem.at[sem], recv_sem=rsem.at[sem], device_id={"dp": c_peer}, device_id_type=MESH
        ).wait_recv()

    def ring(slot, forward_own, step_work):
        right = {"dp": at((z + 1) % 8, x, h, c)}
        left = {"dp": at((z + 7) % 8, x, h, c)}
        other = {"dp": c_peer}
        names = {}

        def name(kind, s, q):
            if (kind, s, q) not in names:
                names[(kind, s, q)] = take()
            return names[(kind, s, q)]

        def goes(kind, s, q):
            return s < 4 or (kind == "r" and q == 0) or (kind == "l" and q == 1)

        def place(kind, s):
            return (z + 8 - s) % 8 if kind == "r" else (z + s) % 8

        def pass_on(kind, s, q):
            target = right if kind == "r" else left
            ref = slot(c, place(kind, s - 1), q)
            send(ref, ref, name(kind, s, q), target)

        def hand(kind, s, q):
            ref = slot(c, place(kind, s), q)
            send(ref, ref, name("f" + kind, s, q), other)

        for q in range(2):
            pass_on("r", 1, q)
            pass_on("l", 1, q)
        if forward_own:
            for q in range(2):
                hand("r", 0, q)
        step_work(0, [(z, 0), (z, 1)], [])
        pending = [("r", 0, 0), ("r", 0, 1)] if forward_own else []
        for s in range(1, 5):
            got = []
            for q in range(2):
                for kind in ("r", "l"):
                    if not goes(kind, s, q):
                        continue
                    arrived(slot(c, place(kind, s), q), name(kind, s, q))
                    if s < 4 and goes(kind, s + 1, q):
                        pass_on(kind, s + 1, q)
                    hand(kind, s, q)
                    got.append((kind, s, q))
            for kind, t, q in pending:
                arrived(slot(1 - c, place(kind, t), q), name("f" + kind, t, q))
            step_work(s, [(place(k, t), q) for k, t, q in got], [(place(k, t), q) for k, t, q in pending])
            pending = got
        for kind, t, q in pending:
            arrived(slot(1 - c, place(kind, t), q), name("f" + kind, t, q))
        step_work(5, [], [(place(k, t), q) for k, t, q in pending])

    scol[8] = qblk[...]
    lane = iota((128, 512), 0)
    col = iota((128, 512), 1)
    for j in range(16):
        perm[pl.ds(128 * j, 128), :] = onehot(col == ((lane // 4) % 8) * 64 + j * 4 + lane % 4)
    acc[...] = jnp.zeros_like(acc)

    pl.semaphore_wait(barrier, 15)
    own = wg.at[c, z, x, h]
    w_h = take()
    send(wblk, own, w_h, {"dp": h_peer})
    wg[c, z, x, h] = wblk[...]
    load_a.wait()
    load_g.wait()

    sel_r = iota((256, 128), 0)
    sel_c = iota((256, 128), 1)

    def prepare(lo, hi):
        def body(part, carry):
            zl = part // 4
            xx = part % 4
            for hh in range(2):
                for cc in range(2):
                    i0 = zl * 16 + xx * 4 + hh * 2 + cc
                    ta = jnp.minimum((76 * i0) // 128, 17)
                    oa = 76 * i0 - 128 * ta
                    tg = jnp.minimum((28 * i0) // 128, 5)
                    og = 28 * i0 - 128 * tg
                    sel_a = onehot((sel_r == sel_c + oa) & (sel_c < 76))
                    sel_g = onehot((sel_r == sel_c - 76 + og) & (sel_c >= 76) & (sel_c < 104))
                    a4 = jnp.concatenate(
                        [av[:, pl.ds(pl.multiple_of((ta + 19 * n) * 128, 128), 256)] for n in range(4)], axis=0
                    )
                    g4 = jnp.concatenate(
                        [gv[:, pl.ds(pl.multiple_of((tg + 7 * n) * 128, 128), 256)] for n in range(4)], axis=0
                    )
                    xa = dot(a4, sel_a).astype(BF16)
                    xg = dot(g4, sel_g).astype(BF16)
                    q = xx // 2
                    off = pl.multiple_of(((xx % 2) * 2 + hh) * 128, 128)
                    for n in range(4):
                        xs[cc, 2 * n + zl, q, 0:128, pl.ds(off, 128)] = xa[128 * n : 128 * n + 128]
                        xs[cc, 2 * n + zl, q, 128:256, pl.ds(off, 128)] = xg[128 * n : 128 * n + 128]
            return carry

        lax.fori_loop(lo, hi, body, 0)

    prepare(0, 2)
    arrived(wg.at[c, z, x, 1 - h], w_h)
    w_x = [take() for _ in range(3)]
    for d in range(3):
        send(wg.at[c, z, x], wg.at[c, z, x], w_x[d], {"dp": x_peers[d]})
    prepare(2, 4)
    for d in range(3):
        arrived(wg.at[c, z, (x + 3 - d) % 4], w_x[d])

    def multiply(color, zz, q):
        w = wg[color, zz, pl.ds(2 * q, 2)]
        wide = jnp.concatenate([w[0, 0], w[0, 1], w[1, 0], w[1, 1]], axis=1)
        acc[...] += dot_nt(xs[color, zz, q], wide)

    def project(s, mine, theirs):
        if s == 0:
            prepare(4, 8)
        for zz, q in mine:
            multiply(c, zz, q)
        for zz, q in theirs:
            multiply(1 - c, zz, q)

    ring(lambda cc, zz, q: wg.at[cc, zz, pl.ds(2 * q, 2)], True, project)

    tok = iota((128, 64), 0)
    length = jnp.zeros((128, 64), jnp.int32)
    for p in range(4):
        length = jnp.where(tok // 32 == p, lens[0, p], length)
    mask = jnp.where(tok % 32 < length, 1.0, 0.0).astype(F32)
    right_proj = acc[0:128].astype(BF16)
    left_proj = (mask * acc[128:256]).astype(BF16)
    row = iota((128, 128), 0)
    colm = iota((128, 128), 1)
    mine = jnp.where(colm // 32 == row % 4, 1.0, 0.0).astype(F32)
    k_row = iota((128, 64), 0)
    k_col = iota((128, 64), 1)
    j_row = iota((64, 128), 0)
    j_col = iota((64, 128), 1)
    total = jnp.zeros((128, 128), F32)
    for par in range(2):
        spread = dot_nt(onehot(k_col == 2 * (k_row // 4) + par), left_proj)
        lefts = (spread * mine).astype(BF16)
        rights = dot(right_proj, onehot(j_col == j_row + 64 * par)).astype(BF16)
        total = total + dot(lefts, rights)
    sketch = total.astype(BF16)
    sk[...] = sketch
    srow[c, x, h] = sketch
    scol[z] = sketch

    s_h = take()
    send(srow.at[c, x, h], srow.at[c, x, h], s_h, {"dp": h_peer})
    s_z = [take() for _ in range(7)]
    for d in range(7):
        send(scol.at[z], scol.at[z], s_z[d], {"dp": z_peers[d]})
    arrived(srow.at[c, x, 1 - h], s_h)
    s_x = [take() for _ in range(3)]
    s_c = [take() for _ in range(4)]
    for d in range(3):
        send(srow.at[c, x], srow.at[c, x], s_x[d], {"dp": x_peers[d]})
    send(srow.at[c, x], srow.at[c, x], s_c[0], {"dp": c_peer})
    for d in range(3):
        xx = (x + 3 - d) % 4
        arrived(srow.at[c, xx], s_x[d])
        send(srow.at[c, xx], srow.at[c, xx], s_c[d + 1], {"dp": c_peer})
    for d in range(7):
        arrived(scol.at[(z + 7 - d) % 8], s_z[d])
    for d in range(4):
        arrived(srow.at[1 - c, (x + 4 - d) % 4], s_c[d])

    gram = jnp.zeros((256, 144), F32)
    for u in range(4):
        rows = [srow[:, :, :, pl.ds(32 * u + 16 * v, 16), :].reshape(256, 128) for v in range(2)]
        cols = [scol[:, pl.ds(32 * u + 16 * v, 16), :].reshape(144, 128) for v in range(2)]
        gram = gram + dot_nt(jnp.concatenate(rows, axis=1), jnp.concatenate(cols, axis=1))
    gr = iota((256, 144), 0)
    gc = iota((256, 144), 1)
    gram = jnp.where((gr // 4) % 4 == (gc // 4) % 4, gram, 0.0)
    pr = iota((64, 256), 0)
    pc = iota((64, 256), 1)
    blk = pc // 16
    pick_rows = onehot(pr == ((blk // 2) % 4) * 16 + (blk % 2) * 8 + (blk // 8) * 4 + pc % 4)
    half = sum(dot(pick_rows, v) for v in pieces(gram))
    nr = iota((144, 256), 0)
    nc = iota((144, 256), 1)
    in_k = (nr < 128) & (nc < 128) & (nc % 32 == (nr // 16) * 4 + nr % 4)
    in_q = (nr >= 128) & (nc >= 128) & ((nc - 128) // 16 == b % 8) & (nc % 4 == nr % 4)
    pick_cols = onehot(in_k | in_q)
    spread = sum(dot(v, pick_cols) for v in pieces(half))
    yr = iota((64, 256), 0)
    yc = iota((64, 256), 1)
    quarter = jnp.where(yc < 128, yc // 32, (yc // 4) % 4) == yr // 16
    spread = jnp.where(quarter, spread, 0.0)
    lx[ly] = spread[0:16] + spread[16:32] + spread[32:48] + spread[48:64]

    l_s = [take() for _ in range(3)]
    for d in range(3):
        send(lx.at[ly], lx.at[ly], l_s[d], {"layer": (ly + 1 + d) % 4})
    for d in range(3):
        arrived(lx.at[(ly + 3 - d) % 4], l_s[d])
    kb[c, x, h] = (lx[0] + lx[1]) + (lx[2] + lx[3])

    k_h = take()
    send(kb.at[c, x, h], kb.at[c, x, h], k_h, {"dp": h_peer})
    arrived(kb.at[c, x, 1 - h], k_h)
    k_x = [take() for _ in range(3)]
    k_c = [take() for _ in range(4)]
    for d in range(3):
        send(kb.at[c, x], kb.at[c, x], k_x[d], {"dp": x_peers[d]})
    send(kb.at[c, x], kb.at[c, x], k_c[0], {"dp": c_peer})
    for d in range(3):
        xx = (x + 3 - d) % 4
        arrived(kb.at[c, xx], k_x[d])
        send(kb.at[c, xx], kb.at[c, xx], k_c[d + 1], {"dp": c_peer})
    for d in range(4):
        arrived(kb.at[1 - c, (x + 4 - d) % 4], k_c[d])

    def tall(v):
        return jnp.concatenate([v, v, v, v], axis=0)

    r4 = iota((64, 128), 0) // 16
    l4 = iota((64, 128), 1)
    wide = []
    side = [jnp.zeros((16, 128), F32), jnp.zeros((16, 128), F32)]
    for j in range(16):
        v = kb[j % 2, j // 4, (j // 2) % 2]
        wide.append(jnp.where(l4 // 32 == r4, tall(v[:, 0:128]), 0.0))
        side[j // 8] = side[j // 8] + v[:, 128:256]
    flat = jnp.concatenate(wide, axis=1)
    part = sum(dot(v, perm[...]) for v in pieces(flat))
    sides = jnp.concatenate([jnp.where((l4 // 4) % 4 == r4, tall(v), 0.0) for v in side], axis=1)
    ir = iota((256, 128), 0)
    ic = iota((256, 128), 1)
    place_q = onehot(ic == (ir // 16) * 4 + ir % 4)
    part_q = sum(dot(v, place_q) for v in pieces(sides))
    for cc in range(2):
        kin[z, cc, :, 0:512] = part[32 * cc : 32 * cc + 32]
        kin[z, cc, :, 512:640] = part_q[32 * cc : 32 * cc + 32]
    ring(lambda cc, zz, q: kin.at[zz, cc, pl.ds(16 * q, 16)], False, lambda s, mine, theirs: None)
    for copy in sent:
        copy.wait_send()


def run_front(act, grd, wblk, qblk, lens):
    vmem = pl.BlockSpec(memory_space=pltpu.VMEM)
    hbm = pl.BlockSpec(memory_space=pl.ANY)
    return pl.pallas_call(
        front,
        out_shape=(jax.ShapeDtypeStruct((128, 128), BF16), jax.ShapeDtypeStruct((8, 2, 32, 640), F32)),
        in_specs=[hbm, hbm, vmem, vmem, pl.BlockSpec(memory_space=pltpu.SMEM)],
        out_specs=(vmem, vmem),
        scratch_shapes=[
            pltpu.VMEM(act.shape, BF16),
            pltpu.VMEM(grd.shape, BF16),
            pltpu.VMEM((2, 8, 2, 256, 512), BF16),
            pltpu.VMEM((2, 8, 4, 2, 64, 128), BF16),
            pltpu.VMEM((2, 4, 2, 128, 128), BF16),
            pltpu.VMEM((9, 128, 128), BF16),
            pltpu.VMEM((4, 16, 256), F32),
            pltpu.VMEM((2, 4, 2, 16, 256), F32),
            pltpu.VMEM((2048, 512), BF16),
            pltpu.VMEM((256, 64), F32),
            pltpu.SemaphoreType.DMA((2,)),
            pltpu.SemaphoreType.DMA((SEMS,)),
            pltpu.SemaphoreType.DMA((SEMS,)),
        ],
        compiler_params=pltpu.CompilerParams(collective_id=0, has_side_effects=True, vmem_limit_bytes=48 * 1024 * 1024),
        name="front",
    )(act, grd, wblk, qblk, lens)


def solve(whole, query_index):
    kernel = whole[:, :512]
    inner = whole[:, 512:576]
    pair_total = kernel.shape[0]
    mean_diag = jnp.trace(kernel) / pair_total
    damping = damp_ratio * mean_diag
    factor = jnp.linalg.cholesky(kernel + damping * jnp.eye(pair_total, dtype=F32))
    solved = jax.scipy.linalg.cho_solve((factor, True), inner)
    own_rows = lax.dynamic_slice_in_dim(solved, lax.axis_index("dp") * 4, 4, 0)
    selected = query_index[:, :, None] == jnp.arange(64, dtype=jnp.int32)[None, None, :]
    picked = jnp.sum(jnp.where(selected, own_rows[:, None, :], jnp.float32(0.0)), axis=-1)
    return jnp.sqrt(mean_diag) * picked


def local(activations, out_grads, in_basis, out_basis, queries, pair_lengths, query_index):
    wblk = jnp.concatenate([in_basis[0].T, out_basis[0].T, jnp.zeros((64, 24), BF16)], axis=1)
    first = (lax.axis_index("dp") % 16) * 4
    qrows = lax.dynamic_slice_in_dim(queries[0], first, 4, 0)
    qblk = qrows.reshape(4, 32, 128).transpose(1, 0, 2).reshape(128, 128)
    sk, kin = run_front(activations[0], out_grads[0], wblk, qblk, pair_lengths)
    sketch = sk.reshape(32, 4, 128).transpose(1, 0, 2).reshape(1, 4, 4096)
    return sketch, solve(kin.reshape(512, 640), query_index)


def solution(mesh):
    placed = (
        P("layer", "dp", None),
        P("layer", "dp", None),
        P("layer", "dp", None),
        P("layer", "dp", None),
        P("layer", None, None),
        P("dp", None),
        P("dp", None),
    )
    return jax.shard_map(
        local,
        mesh=mesh,
        in_specs=placed,
        out_specs=(P("layer", "dp", None), P("dp", None)),
        check_vma=False,
    )
```

```python
import jax
import jax.numpy as jnp
from jax import lax
from jax.experimental import pallas as pl
from jax.experimental.pallas import tpu as pltpu
from jax.sharding import PartitionSpec as P

MESH = pl.DeviceIdType.MESH
damp_ratio = 0.5
F32 = jnp.float32
BF16 = jnp.bfloat16
NT = (((1,), (1,)), ((), ()))
SEMS = 160


def iota(shape, dim):
    return lax.broadcasted_iota(jnp.int32, shape, dim)


def onehot(cond):
    return jnp.where(cond, 1.0, 0.0).astype(BF16)


def pieces(v):
    hi = v.astype(BF16)
    rest = v - hi.astype(F32)
    mid = rest.astype(BF16)
    return hi, mid, (rest - mid.astype(F32)).astype(BF16)


def dot(a, b):
    return jnp.dot(a, b, preferred_element_type=F32)


def dot_nt(a, b):
    return lax.dot_general(a, b, NT, preferred_element_type=F32)


def front(act, grd, inb_hbm, outb_hbm, qry_hbm, lens_hbm, sk, kin, av, gv, inb, outb, qry, lens, xs, wa, wb, srow, scol, lx, kb, perm, acc, in_sem, ssem, rsem):
    me = lax.axis_index("dp")
    ly = lax.axis_index("layer")
    c = me % 2
    h = (me // 2) % 2
    x = (me // 4) % 4
    z = me // 16
    b = me % 16

    def at(zz, xx, hh, cc):
        return ((zz * 4 + xx) * 2 + hh) * 2 + cc

    h_peer = at(z, x, 1 - h, c)
    c_peer = at(z, x, h, 1 - c)
    x_peers = [at(z, (x + d) % 4, h, c) for d in range(1, 4)]
    z_peers = [at((z + d) % 8, x, h, c) for d in range(1, 8)]

    load_a = pltpu.make_async_copy(act, av, in_sem.at[0])
    load_g = pltpu.make_async_copy(grd, gv, in_sem.at[1])
    load_l = pltpu.make_async_copy(lens_hbm, lens, in_sem.at[2])
    load_i = pltpu.make_async_copy(inb_hbm, inb, in_sem.at[3])
    load_o = pltpu.make_async_copy(outb_hbm, outb, in_sem.at[4])
    load_q = pltpu.make_async_copy(qry_hbm, qry, in_sem.at[5])
    for load in (load_i, load_o, load_a, load_g, load_q, load_l):
        load.start()

    barrier = pltpu.get_barrier_semaphore()
    for peer in [h_peer, c_peer] + x_peers + z_peers:
        pl.semaphore_signal(barrier, inc=1, device_id={"dp": peer}, device_id_type=MESH)
    for d in range(1, 4):
        for hh in range(2):
            peer = {"dp": at(z, x, (h + hh) % 2, c), "layer": (ly + d) % 4}
            pl.semaphore_signal(barrier, inc=1, device_id=peer, device_id_type=MESH)

    used = [0]
    sent = []

    def take():
        used[0] += 1
        return used[0] - 1

    def send(src, dst, sem, device):
        copy = pltpu.make_async_remote_copy(
            src_ref=src, dst_ref=dst, send_sem=ssem.at[sem], recv_sem=rsem.at[sem], device_id=device, device_id_type=MESH
        )
        copy.start()
        sent.append(copy)

    def arrived(slot, sem):
        pltpu.make_async_remote_copy(
            src_ref=slot, dst_ref=slot, send_sem=ssem.at[sem], recv_sem=rsem.at[sem], device_id={"dp": c_peer}, device_id_type=MESH
        ).wait_recv()

    def ring(slot, forward_own, step_work):
        right = {"dp": at((z + 1) % 8, x, h, c)}
        left = {"dp": at((z + 7) % 8, x, h, c)}
        other = {"dp": c_peer}
        names = {}

        def name(kind, s, q):
            if (kind, s, q) not in names:
                names[(kind, s, q)] = take()
            return names[(kind, s, q)]

        def goes(kind, s, q):
            return s < 4 or (kind == "r" and q == 0) or (kind == "l" and q == 1)

        def place(kind, s):
            return (z + 8 - s) % 8 if kind == "r" else (z + s) % 8

        def pass_on(kind, s, q):
            target = right if kind == "r" else left
            ref = slot(c, place(kind, s - 1), q)
            send(ref, ref, name(kind, s, q), target)

        def hand(kind, s, q):
            ref = slot(c, place(kind, s), q)
            send(ref, ref, name("f" + kind, s, q), other)

        for q in range(2):
            pass_on("r", 1, q)
            pass_on("l", 1, q)
        if forward_own:
            for q in range(2):
                hand("r", 0, q)
        step_work(0, [(z, 0), (z, 1)], [])
        pending = [("r", 0, 0), ("r", 0, 1)] if forward_own else []
        for s in range(1, 5):
            got = []
            for q in range(2):
                for kind in ("r", "l"):
                    if not goes(kind, s, q):
                        continue
                    arrived(slot(c, place(kind, s), q), name(kind, s, q))
                    if s < 4 and goes(kind, s + 1, q):
                        pass_on(kind, s + 1, q)
                    hand(kind, s, q)
                    got.append((kind, s, q))
            for kind, t, q in pending:
                arrived(slot(1 - c, place(kind, t), q), name("f" + kind, t, q))
            step_work(s, [(place(k, t), q) for k, t, q in got], [(place(k, t), q) for k, t, q in pending])
            pending = got
        for kind, t, q in pending:
            arrived(slot(1 - c, place(kind, t), q), name("f" + kind, t, q))
        step_work(5, [], [(place(k, t), q) for k, t, q in pending])

    eye = onehot(iota((64, 64), 0) == iota((64, 64), 1))
    load_i.wait()
    load_o.wait()
    out_t = dot_nt(eye, outb[...]).astype(BF16)
    in_at = onehot(iota((76, 128), 0) == iota((76, 128), 1))
    out_at = onehot(iota((28, 128), 0) + 76 == iota((28, 128), 1))
    own = (dot(inb[...], in_at) + dot(out_t, out_at)).astype(BF16)

    @pl.when(c == 0)
    def _():
        wa[z, x, h] = own

    @pl.when(c == 1)
    def _():
        wb[x, h, z] = own

    def tables():
        load_q.wait()
        q_row = iota((8, 64), 0)
        q_col = iota((8, 64), 1)
        low = onehot((q_row < 4) & (q_col == 4 * b + q_row))
        high = onehot((q_row >= 4) & (q_col == 4 * b + q_row - 4))
        tiles = [
            dot(low, qry[:, 256 * i : 256 * i + 128]) + dot(high, qry[:, 256 * i + 128 : 256 * i + 256]) for i in range(16)
        ]
        scol[8] = jnp.concatenate(tiles, axis=0).astype(BF16)
        lane = iota((128, 512), 0)
        col = iota((128, 512), 1)
        for j in range(16):
            perm[pl.ds(128 * j, 128), :] = onehot(col == ((lane // 4) % 8) * 64 + j * 4 + lane % 4)
        load_l.wait()
        load_a.wait()
        load_g.wait()

    acc[...] = jnp.zeros_like(acc)

    sel_r = iota((256, 128), 0)
    sel_c = iota((256, 128), 1)

    def prepare(lo, hi):
        def body(part, carry):
            zl = part // 4
            xx = part % 4
            for hh in range(2):
                for cc in range(2):
                    i0 = zl * 16 + xx * 4 + hh * 2 + cc
                    ta = jnp.minimum((76 * i0) // 128, 17)
                    oa = 76 * i0 - 128 * ta
                    tg = jnp.minimum((28 * i0) // 128, 5)
                    og = 28 * i0 - 128 * tg
                    sel_a = onehot((sel_r == sel_c + oa) & (sel_c < 76))
                    sel_g = onehot((sel_r == sel_c - 76 + og) & (sel_c >= 76) & (sel_c < 104))
                    a4 = jnp.concatenate(
                        [av[:, pl.ds(pl.multiple_of((ta + 19 * n) * 128, 128), 256)] for n in range(4)], axis=0
                    )
                    g4 = jnp.concatenate(
                        [gv[:, pl.ds(pl.multiple_of((tg + 7 * n) * 128, 128), 256)] for n in range(4)], axis=0
                    )
                    xa = dot(a4, sel_a).astype(BF16)
                    xg = dot(g4, sel_g).astype(BF16)
                    for n in range(4):
                        xs[cc, 2 * n + zl, xx, 0:128, 128 * hh : 128 * hh + 128] = xa[128 * n : 128 * n + 128]
                        xs[cc, 2 * n + zl, xx, 128:256, 128 * hh : 128 * hh + 128] = xg[128 * n : 128 * n + 128]
            return carry

        lax.fori_loop(lo, hi, body, 0)

    def multiply_a(zz, x0, count):
        for i in range(count):
            w = jnp.concatenate([wa[zz, x0 + i, 0], wa[zz, x0 + i, 1]], axis=1)
            acc[...] += dot_nt(xs[0, zz, x0 + i], w)

    def multiply_b(xx):
        def body(i, carry):
            for zz in (2 * i, 2 * i + 1):
                w = jnp.concatenate([wb[xx, 0, zz], wb[xx, 1, zz]], axis=1)
                acc[...] += dot_nt(xs[1, zz, xx], w)
            return carry

        lax.fori_loop(0, 4, body, 0)

    pl.semaphore_wait(barrier, 18)
    hand_a = {("r", 0, 0): take(), ("r", 0, 1): take()}
    pass_a = {}
    for s in range(1, 5):
        for kind, q in (("r", 0), ("l", 0), ("r", 1), ("l", 1)):
            if s < 4 or (kind, q) in (("r", 0), ("l", 1)):
                hand_a[(kind, s, q)] = take()
                pass_a[(kind, s, q)] = take()
    hand_b = {(n, q): take() for n in ("own", "left", "right", "far") for q in range(2)}
    pass_b = {n: take() for n in ("r0", "r1", "l0", "l1", "far0", "far1")}
    first = [take() for _ in range(15)]

    def place(kind, s):
        return (z + 8 - s) % 8 if kind == "r" else (z + s) % 8

    def slot_a(zz, q):
        return wa.at[zz, pl.ds(2 * q, 2)]

    far = (x + 2) % 4
    place_b = {"own": x, "left": (x + 3) % 4, "right": (x + 1) % 4, "far": far}
    other = {"dp": c_peer}

    @pl.when(c == 0)
    def _():
        base = len(sent)
        ref = wa.at[z, x, h]
        for i, peer in enumerate([h_peer] + x_peers):
            send(ref, ref, first[i], {"dp": peer})
        tables()
        for d in range(3):
            ref = wa.at[z, (x + 3 - d) % 4, h]
            arrived(ref, first[1 + d])
            send(ref, ref, first[4 + d], {"dp": h_peer})
        prepare(0, 2)
        arrived(wa.at[z, x, 1 - h], first[0])
        for d in range(3):
            arrived(wa.at[z, (x + 3 - d) % 4, 1 - h], first[4 + d])
        right = {"dp": at((z + 1) % 8, x, h, c)}
        left = {"dp": at((z + 7) % 8, x, h, c)}

        def pass_on(kind, s, q):
            ref = slot_a(place(kind, s - 1), q)
            send(ref, ref, pass_a[(kind, s, q)], right if kind == "r" else left)

        def hand(kind, s, q):
            ref = slot_a(place(kind, s), q)
            send(ref, ref, hand_a[(kind, s, q)], other)

        for kind, q in (("r", 0), ("l", 1), ("r", 1), ("l", 0)):
            pass_on(kind, 1, q)
        hand("r", 0, 0)
        hand("r", 0, 1)
        prepare(2, 8)
        todo = [(z, 0), (z, 1)]
        for s in range(1, 5):
            ready = []
            for kind, q in (("r", 0), ("l", 1), ("r", 1), ("l", 0)):
                if (kind, s, q) not in pass_a:
                    continue
                arrived(slot_a(place(kind, s), q), pass_a[(kind, s, q)])
                if (kind, s + 1, q) in pass_a:
                    pass_on(kind, s + 1, q)
                hand(kind, s, q)
                ready.append((place(kind, s), q))
            for zz, q in todo:
                multiply_a(zz, 2 * q, 2)
            todo = ready
        for zz, q in todo:
            multiply_a(zz, 2 * q, 2)
        for n in ("own", "left", "right", "far"):
            for q in range(2):
                arrived(wb.at[place_b[n], q], hand_b[(n, q)])
            multiply_b(place_b[n])
        for copy in sent[base:]:
            copy.wait_send()
        del sent[base:]

    @pl.when(c == 1)
    def _():
        base = len(sent)
        ref = wb.at[x, h, z]
        for i, peer in enumerate([h_peer] + z_peers):
            send(ref, ref, first[i], {"dp": peer})
        tables()
        for d in (0, 6, 1, 5, 2, 4, 3):
            ref = wb.at[x, h, (z + 7 - d) % 8]
            arrived(ref, first[1 + d])
            send(ref, ref, first[8 + d], {"dp": h_peer})
        prepare(0, 3)
        arrived(wb.at[x, 1 - h, z], first[0])
        for d in range(7):
            arrived(wb.at[x, 1 - h, (z + 7 - d) % 8], first[8 + d])
        right = {"dp": x_peers[0]}
        left = {"dp": x_peers[2]}
        for name, q, target in (("r0", 0, right), ("l1", 1, left), ("r1", 1, right), ("l0", 0, left)):
            send(wb.at[x, q], wb.at[x, q], pass_b[name], target)
        for q in range(2):
            send(wb.at[x, q], wb.at[x, q], hand_b[("own", q)], other)
        prepare(3, 8)
        xl, xr = place_b["left"], place_b["right"]
        arrived(wb.at[xl, 0], pass_b["r0"])
        send(wb.at[xl, 0], wb.at[xl, 0], pass_b["far0"], right)
        send(wb.at[xl, 0], wb.at[xl, 0], hand_b[("left", 0)], other)
        arrived(wb.at[xr, 1], pass_b["l1"])
        send(wb.at[xr, 1], wb.at[xr, 1], pass_b["far1"], left)
        send(wb.at[xr, 1], wb.at[xr, 1], hand_b[("right", 1)], other)
        multiply_b(x)
        arrived(wb.at[xl, 1], pass_b["r1"])
        send(wb.at[xl, 1], wb.at[xl, 1], hand_b[("left", 1)], other)
        arrived(wb.at[xr, 0], pass_b["l0"])
        send(wb.at[xr, 0], wb.at[xr, 0], hand_b[("right", 0)], other)
        multiply_b(xl)
        arrived(wb.at[far, 0], pass_b["far0"])
        send(wb.at[far, 0], wb.at[far, 0], hand_b[("far", 0)], other)
        arrived(wb.at[far, 1], pass_b["far1"])
        send(wb.at[far, 1], wb.at[far, 1], hand_b[("far", 1)], other)
        multiply_b(xr)
        multiply_b(far)
        for s in range(5):
            for kind, q in (("r", 0), ("l", 1), ("r", 1), ("l", 0)):
                if (kind, s, q) not in hand_a:
                    continue
                arrived(slot_a(place(kind, s), q), hand_a[(kind, s, q)])
                multiply_a(place(kind, s), 2 * q, 2)
        for copy in sent[base:]:
            copy.wait_send()
        del sent[base:]

    tok = iota((128, 64), 0)
    length = jnp.zeros((128, 64), jnp.int32)
    for p in range(4):
        length = jnp.where(tok // 32 == p, lens[0, p], length)
    mask = jnp.where(tok % 32 < length, 1.0, 0.0).astype(F32)
    right_proj = acc[0:128].astype(BF16)
    left_proj = (mask * acc[128:256]).astype(BF16)
    row = iota((128, 128), 0)
    colm = iota((128, 128), 1)
    mine = jnp.where(colm // 32 == row % 4, 1.0, 0.0).astype(F32)
    k_row = iota((128, 64), 0)
    k_col = iota((128, 64), 1)
    j_row = iota((64, 128), 0)
    j_col = iota((64, 128), 1)
    total = jnp.zeros((128, 128), F32)
    for par in range(2):
        spread = dot_nt(onehot(k_col == 2 * (k_row // 4) + par), left_proj)
        lefts = (spread * mine).astype(BF16)
        rights = dot(right_proj, onehot(j_col == j_row + 64 * par)).astype(BF16)
        total = total + dot(lefts, rights)
    sketch = total.astype(BF16)
    sk[...] = sketch
    srow[c, x, h] = sketch
    scol[z] = sketch

    s_h = take()
    send(srow.at[c, x, h], srow.at[c, x, h], s_h, {"dp": h_peer})
    s_z = [take() for _ in range(7)]
    for d in range(7):
        send(scol.at[z], scol.at[z], s_z[d], {"dp": z_peers[d]})
    arrived(srow.at[c, x, 1 - h], s_h)
    s_x = [take() for _ in range(3)]
    s_c = [take() for _ in range(4)]
    for d in range(3):
        send(srow.at[c, x], srow.at[c, x], s_x[d], {"dp": x_peers[d]})
    send(srow.at[c, x], srow.at[c, x], s_c[0], {"dp": c_peer})
    for d in range(3):
        xx = (x + 3 - d) % 4
        arrived(srow.at[c, xx], s_x[d])
        send(srow.at[c, xx], srow.at[c, xx], s_c[d + 1], {"dp": c_peer})
    for d in range(7):
        arrived(scol.at[(z + 7 - d) % 8], s_z[d])
    for d in range(4):
        arrived(srow.at[1 - c, (x + 4 - d) % 4], s_c[d])

    gram = jnp.zeros((256, 144), F32)
    for u in range(4):
        rows = [srow[:, :, :, pl.ds(32 * u + 16 * v, 16), :].reshape(256, 128) for v in range(2)]
        cols = [scol[:, pl.ds(32 * u + 16 * v, 16), :].reshape(144, 128) for v in range(2)]
        gram = gram + dot_nt(jnp.concatenate(rows, axis=1), jnp.concatenate(cols, axis=1))
    gr = iota((256, 144), 0)
    gc = iota((256, 144), 1)
    gram = jnp.where((gr // 4) % 4 == (gc // 4) % 4, gram, 0.0)
    pr = iota((64, 256), 0)
    pc = iota((64, 256), 1)
    blk = pc // 16
    pick_rows = onehot(pr == ((blk // 2) % 4) * 16 + (blk % 2) * 8 + (blk // 8) * 4 + pc % 4)
    half = sum(dot(pick_rows, v) for v in pieces(gram))
    nr = iota((144, 256), 0)
    nc = iota((144, 256), 1)
    in_k = (nr < 128) & (nc < 128) & (nc % 32 == (nr // 16) * 4 + nr % 4)
    in_q = (nr >= 128) & (nc >= 128) & ((nc - 128) // 16 == b % 8) & (nc % 4 == nr % 4)
    pick_cols = onehot(in_k | in_q)
    spread = sum(dot(v, pick_cols) for v in pieces(half))
    yr = iota((64, 256), 0)
    yc = iota((64, 256), 1)
    quarter = jnp.where(yc < 128, yc // 32, (yc // 4) % 4) == yr // 16
    spread = jnp.where(quarter, spread, 0.0)
    lx[h, ly] = spread[0:16] + spread[16:32] + spread[32:48] + spread[48:64]

    l_s = [(d, hh, take()) for d in range(4) for hh in range(2) if d + hh > 0]
    for d, hh, sem in l_s:
        peer = {"dp": at(z, x, (h + hh) % 2, c), "layer": (ly + d) % 4}
        send(lx.at[h, ly], lx.at[h, ly], sem, peer)
    for d, hh, sem in l_s:
        arrived(lx.at[(h + hh) % 2, (ly + 4 - d) % 4], sem)
    for hh in range(2):
        kb[c, x, hh] = (lx[hh, 0] + lx[hh, 1]) + (lx[hh, 2] + lx[hh, 3])
    k_x = [take() for _ in range(3)]
    k_c = [take() for _ in range(4)]
    for d in range(3):
        send(kb.at[c, x], kb.at[c, x], k_x[d], {"dp": x_peers[d]})
    send(kb.at[c, x], kb.at[c, x], k_c[0], {"dp": c_peer})
    for d in range(3):
        xx = (x + 3 - d) % 4
        arrived(kb.at[c, xx], k_x[d])
        send(kb.at[c, xx], kb.at[c, xx], k_c[d + 1], {"dp": c_peer})
    for d in range(4):
        arrived(kb.at[1 - c, (x + 4 - d) % 4], k_c[d])

    def tall(v):
        return jnp.concatenate([v, v, v, v], axis=0)

    r4 = iota((64, 128), 0) // 16
    l4 = iota((64, 128), 1)
    wide = []
    side = [jnp.zeros((16, 128), F32), jnp.zeros((16, 128), F32)]
    for j in range(16):
        v = kb[j % 2, j // 4, (j // 2) % 2]
        wide.append(jnp.where(l4 // 32 == r4, tall(v[:, 0:128]), 0.0))
        side[j // 8] = side[j // 8] + v[:, 128:256]
    flat = jnp.concatenate(wide, axis=1)
    part = sum(dot(v, perm[...]) for v in pieces(flat))
    sides = jnp.concatenate([jnp.where((l4 // 4) % 4 == r4, tall(v), 0.0) for v in side], axis=1)
    ir = iota((256, 128), 0)
    ic = iota((256, 128), 1)
    place_q = onehot(ic == (ir // 16) * 4 + ir % 4)
    part_q = sum(dot(v, place_q) for v in pieces(sides))
    for cc in range(2):
        kin[z, cc, :, 0:512] = part[32 * cc : 32 * cc + 32]
        kin[z, cc, :, 512:640] = part_q[32 * cc : 32 * cc + 32]
    ring(lambda cc, zz, q: kin.at[zz, cc, pl.ds(16 * q, 16)], False, lambda s, mine, theirs: None)
    for copy in sent:
        copy.wait_send()


def run_front(act, grd, inb, outb, qry, lens):
    vmem = pl.BlockSpec(memory_space=pltpu.VMEM)
    hbm = pl.BlockSpec(memory_space=pltpu.HBM)
    return pl.pallas_call(
        front,
        out_shape=(jax.ShapeDtypeStruct((128, 128), BF16), jax.ShapeDtypeStruct((8, 2, 32, 640), F32)),
        in_specs=[hbm] * 6,
        out_specs=(vmem, vmem),
        scratch_shapes=[
            pltpu.VMEM(act.shape, BF16),
            pltpu.VMEM(grd.shape, BF16),
            pltpu.VMEM(inb.shape, BF16),
            pltpu.VMEM(outb.shape, BF16),
            pltpu.VMEM(qry.shape, BF16),
            pltpu.SMEM((1, 4), jnp.int32),
            pltpu.VMEM((2, 8, 4, 256, 256), BF16),
            pltpu.VMEM((8, 4, 2, 64, 128), BF16),
            pltpu.VMEM((4, 2, 8, 64, 128), BF16),
            pltpu.VMEM((2, 4, 2, 128, 128), BF16),
            pltpu.VMEM((9, 128, 128), BF16),
            pltpu.VMEM((2, 4, 16, 256), F32),
            pltpu.VMEM((2, 4, 2, 16, 256), F32),
            pltpu.VMEM((2048, 512), BF16),
            pltpu.VMEM((256, 64), F32),
            pltpu.SemaphoreType.DMA((6,)),
            pltpu.SemaphoreType.DMA((SEMS,)),
            pltpu.SemaphoreType.DMA((SEMS,)),
        ],
        compiler_params=pltpu.CompilerParams(collective_id=0, has_side_effects=True, vmem_limit_bytes=48 * 1024 * 1024),
        name="front",
    )(*[pltpu.with_memory_space_constraint(v, pltpu.HBM) for v in (act, grd, inb, outb, qry, lens)])


HIGH = lax.Precision.HIGHEST


STRIP = 32


def invert(d):
    sub = iota((8, 128), 0)
    lane = iota((8, 128), 1)
    big_row = iota((128, 128), 0) // STRIP
    big_col = iota((128, 128), 1) // STRIP
    per = STRIP // 8
    for s in range(128 // STRIP):
        rows = [d[8 * i : 8 * i + 8, :] for i in range(s * per, s * per + per)]
        for p in range(per):
            first = s * STRIP + 8 * p
            inside = lane // 8 == first // 8
            head = rows[p]
            cols = [jnp.broadcast_to(head[:, first + k : first + k + 1], (8, 128)) for k in range(8)]
            head = jnp.where(inside, jnp.where(lane % 8 == sub, 1.0, 0.0), head)
            for k in range(8):
                here = sub == k
                f = cols[k]
                pivot = 1.0 / f[k : k + 1, :]
                lead = head[k : k + 1, :] * pivot
                head = jnp.where(here, lead, head - f * lead)
                for j in range(k + 1, 8):
                    g = cols[j][k : k + 1, :] * pivot
                    cols[j] = jnp.where(here, g, cols[j] - f * g)
            leads = [jnp.broadcast_to(head[k : k + 1, :], (8, 128)) for k in range(8)]
            for i in range(per):
                if i == p:
                    continue
                v = rows[i]
                r = jnp.where(inside, 0.0, v)
                for k in range(8):
                    r = r - v[:, first + k : first + k + 1] * leads[k]
                rows[i] = r
            rows[p] = head
        done = jnp.concatenate(rows, axis=0)
        zero = jnp.zeros((STRIP, 128), F32)
        placed = jnp.concatenate([done if t == s else zero for t in range(128 // STRIP)], axis=0)
        side = jnp.where((big_col == s) & (big_row != s), d, 0.0)
        keep = jnp.where(big_col == s, 0.0, d)
        keep = jnp.where(big_row == s, placed, keep)
        d = keep - jnp.dot(side, placed, precision=HIGH, preferred_element_type=F32)
    return d


def solver(sk, whole, qidx_hbm, sketch, scores, a, qidx, sem):
    load = pltpu.make_async_copy(qidx_hbm, qidx, sem)
    load.start()
    flat = sk[...].astype(F32)
    for m in range(32):
        sketch[:, 128 * m : 128 * m + 128] = flat[4 * m : 4 * m + 4].astype(BF16)
    a[...] = whole[...]
    row = iota((128, 128), 0)
    col = iota((128, 128), 1)
    diag = jnp.zeros((128, 128), F32)
    for j in range(4):
        diag = diag + jnp.where(row == col, whole[128 * j : 128 * j + 128, 128 * j : 128 * j + 128], 0.0)
    mean_diag = jnp.sum(diag) / 512.0
    damping = damp_ratio * mean_diag

    def step(j, carry):
        at = pl.multiple_of(j * 128, 128)
        block = a[pl.ds(at, 128), pl.ds(at, 128)] + jnp.where(row == col, damping, 0.0)
        inv = invert(block)
        for n in range(4):

            @pl.when(j == n)
            def _():
                lo = 128 * n
                hi = lo + 128
                lead = jnp.dot(inv, a[lo:hi, hi:640], precision=HIGH, preferred_element_type=F32)
                a[lo:hi, hi:640] = lead
                if n < 3:
                    a[hi:512, hi:640] -= jnp.dot(a[hi:512, lo:hi], lead, precision=HIGH, preferred_element_type=F32)

        return carry

    lax.fori_loop(0, 4, step, 0)
    for n in range(2, -1, -1):
        lo = 128 * n
        hi = lo + 128
        a[lo:hi, 512:640] -= jnp.dot(a[lo:hi, hi:512], a[hi:512, 512:640], precision=HIGH, preferred_element_type=F32)
    me = lax.axis_index("dp")
    pick = jnp.where(iota((8, 512), 1) == me * 4 + iota((8, 512), 0), 1.0, 0.0).astype(F32)
    own = jnp.dot(pick, a[:, 512:640], precision=HIGH, preferred_element_type=F32)[0:4]
    load.wait()
    lanes = iota((4, 128), 1)
    spot = iota((4, 8), 1)
    out = jnp.zeros((4, 8), F32)
    for s in range(8):
        chosen = jnp.sum(jnp.where(lanes == qidx[:, s : s + 1], own, 0.0), axis=1, keepdims=True)
        out = jnp.where(spot == s, chosen, out)
    scores[...] = jnp.sqrt(mean_diag) * out


def solve(sk, whole, query_index):
    vmem = pl.BlockSpec(memory_space=pltpu.VMEM)
    return pl.pallas_call(
        solver,
        out_shape=(jax.ShapeDtypeStruct((4, 4096), BF16), jax.ShapeDtypeStruct((4, 8), F32)),
        in_specs=[vmem, vmem, pl.BlockSpec(memory_space=pltpu.HBM)],
        out_specs=(vmem, vmem),
        scratch_shapes=[pltpu.VMEM((512, 640), F32), pltpu.VMEM((4, 8), jnp.int32), pltpu.SemaphoreType.DMA],
        compiler_params=pltpu.CompilerParams(vmem_limit_bytes=32 * 1024 * 1024),
        name="solver",
    )(sk, whole, pltpu.with_memory_space_constraint(query_index, pltpu.HBM))


def local(activations, out_grads, in_basis, out_basis, queries, pair_lengths, query_index):
    sk, kin = run_front(
        activations[0], out_grads[0], in_basis[0].T, out_basis[0], queries[0], pair_lengths
    )
    sketch, scores = solve(sk, kin.reshape(512, 640), query_index)
    return sketch[None], scores


def solution(mesh):
    placed = (
        P("layer", "dp", None),
        P("layer", "dp", None),
        P("layer", "dp", None),
        P("layer", "dp", None),
        P("layer", None, None),
        P("dp", None),
        P("dp", None),
    )
    return jax.shard_map(
        local,
        mesh=mesh,
        in_specs=placed,
        out_specs=(P("layer", "dp", None), P("dp", None)),
        check_vma=False,
    )
```

```python
import jax
import jax.numpy as jnp
from jax import lax
from jax.experimental import pallas as pl
from jax.experimental.pallas import tpu as pltpu
from jax.sharding import PartitionSpec as P

MESH = pl.DeviceIdType.MESH
damp_ratio = 0.5
F32 = jnp.float32
BF16 = jnp.bfloat16
NT = (((1,), (1,)), ((), ()))
SEMS = 192


def iota(shape, dim):
    return lax.broadcasted_iota(jnp.int32, shape, dim)


def onehot(cond):
    return jnp.where(cond, 1.0, 0.0).astype(BF16)


def pieces(v):
    hi = v.astype(BF16)
    rest = v - hi.astype(F32)
    mid = rest.astype(BF16)
    return hi, mid, (rest - mid.astype(F32)).astype(BF16)


def dot(a, b):
    return jnp.dot(a, b, preferred_element_type=F32)


def dot_nt(a, b):
    return lax.dot_general(a, b, NT, preferred_element_type=F32)


HIGH = lax.Precision.HIGHEST


STRIP = 64
PANEL = 16
PV = 2


def invert(d, between):
    sub = iota((8, 128), 0)
    lane = iota((8, 128), 1)
    big_row = iota((STRIP, 128), 0)
    big_col = iota((STRIP, 128), 1) // STRIP
    per = STRIP // 8
    count = 128 // STRIP
    strips = [d[STRIP * s : STRIP * s + STRIP, :] for s in range(count)]
    for s in range(count):
        rows = [strips[s][8 * i : 8 * i + 8, :] for i in range(per)]
        for p in range(0, per, PV):
            first = s * STRIP + 8 * p
            inside = lane // PANEL == first // PANEL
            heads = rows[p : p + PV]
            cols = [[jnp.broadcast_to(v[:, first + k : first + k + 1], (8, 128)) for v in heads] for k in range(PANEL)]
            heads = [
                jnp.where(inside, jnp.where(lane % PANEL == sub + 8 * n, 1.0, 0.0), v) for n, v in enumerate(heads)
            ]
            for k in range(PANEL):
                n0, r0 = k // 8, k % 8
                here = sub == r0
                f = cols[k]
                pivot = 1.0 / f[n0][r0 : r0 + 1, :]
                for j in range(k + 1, PANEL):
                    g = cols[j][n0][r0 : r0 + 1, :] * pivot
                    cols[j] = [
                        jnp.where(here, g, v - f[n] * g) if n == n0 else v - f[n] * g for n, v in enumerate(cols[j])
                    ]
                lead = heads[n0][r0 : r0 + 1, :] * pivot
                heads = [
                    jnp.where(here, lead, v - f[n] * lead) if n == n0 else v - f[n] * lead for n, v in enumerate(heads)
                ]
            rows[p : p + PV] = heads
            others = [i for i in range(per) if not p <= i < p + PV]
            if others:
                leads = [jnp.broadcast_to(heads[k // 8][k % 8 : k % 8 + 1, :], (8, 128)) for k in range(PANEL)]
                for i in others:
                    v = rows[i]
                    r = jnp.where(inside, 0.0, v)
                    for k in range(PANEL):
                        r = r - v[:, first + k : first + k + 1] * leads[k]
                    rows[i] = r
        done = jnp.concatenate(rows, axis=0) if per > 1 else rows[0]
        zero = jnp.zeros((STRIP, 128), F32)
        placed = jnp.concatenate([done if t == s else zero for t in range(count)], axis=0)
        new = [None] * count
        new[s] = done
        for t in [(s + i) % count for i in range(1, count)]:
            v = strips[t]
            side = jnp.where(big_col == s, v, 0.0)
            keep = jnp.where(big_col == s, 0.0, v)
            new[t] = keep - jnp.dot(side, placed, precision=HIGH, preferred_element_type=F32)
        strips = new
        if s == 0:
            between()
    return jnp.concatenate(strips, axis=0)


def front(act, grd, inb_hbm, outb_hbm, qry_hbm, lens_hbm, qidx_hbm, sk, scores, kin, a, tz, tl, qidx, av, gv, inb, outb, qry, lens, xs, wa, wb, srow, scol, lx, kb, perm, acc, in_sem, ssem, rsem):
    me = lax.axis_index("dp")
    ly = lax.axis_index("layer")
    c = me % 2
    h = (me // 2) % 2
    x = (me // 4) % 4
    z = me // 16
    b = me % 16

    def at(zz, xx, hh, cc):
        return ((zz * 4 + xx) * 2 + hh) * 2 + cc

    h_peer = at(z, x, 1 - h, c)
    c_peer = at(z, x, h, 1 - c)
    x_peers = [at(z, (x + d) % 4, h, c) for d in range(1, 4)]
    z_peers = [at((z + d) % 8, x, h, c) for d in range(1, 8)]

    load_a = pltpu.make_async_copy(act, av, in_sem.at[0])
    load_g = pltpu.make_async_copy(grd, gv, in_sem.at[1])
    load_l = pltpu.make_async_copy(lens_hbm, lens, in_sem.at[2])
    load_i = pltpu.make_async_copy(inb_hbm, inb, in_sem.at[3])
    load_o = pltpu.make_async_copy(outb_hbm, outb, in_sem.at[4])
    load_q = pltpu.make_async_copy(qry_hbm, qry, in_sem.at[5])
    load_x = pltpu.make_async_copy(qidx_hbm, qidx, in_sem.at[6])
    for load in (load_i, load_o, load_a, load_g, load_q, load_l, load_x):
        load.start()

    barrier = pltpu.get_barrier_semaphore()
    for peer in [h_peer, c_peer] + x_peers + z_peers:
        pl.semaphore_signal(barrier, inc=1, device_id={"dp": peer}, device_id_type=MESH)
    for d in range(1, 4):
        for hh in range(2):
            peer = {"dp": at(z, x, (h + hh) % 2, c), "layer": (ly + d) % 4}
            pl.semaphore_signal(barrier, inc=1, device_id=peer, device_id_type=MESH)

    used = [0]
    sent = []

    def take():
        used[0] += 1
        return used[0] - 1

    def send(src, dst, sem, device):
        copy = pltpu.make_async_remote_copy(
            src_ref=src, dst_ref=dst, send_sem=ssem.at[sem], recv_sem=rsem.at[sem], device_id=device, device_id_type=MESH
        )
        copy.start()
        sent.append(copy)

    def arrived(slot, sem):
        pltpu.make_async_remote_copy(
            src_ref=slot, dst_ref=slot, send_sem=ssem.at[sem], recv_sem=rsem.at[sem], device_id={"dp": c_peer}, device_id_type=MESH
        ).wait_recv()

    eye = onehot(iota((64, 64), 0) == iota((64, 64), 1))
    load_i.wait()
    load_o.wait()
    out_t = dot_nt(eye, outb[...]).astype(BF16)
    in_at = onehot(iota((76, 128), 0) == iota((76, 128), 1))
    out_at = onehot(iota((28, 128), 0) + 76 == iota((28, 128), 1))
    own = (dot(inb[...], in_at) + dot(out_t, out_at)).astype(BF16)

    @pl.when(c == 0)
    def _():
        wa[z, x, h] = own

    @pl.when(c == 1)
    def _():
        wb[x, h, z] = own

    def tables():
        load_q.wait()
        q_row = iota((8, 64), 0)
        q_col = iota((8, 64), 1)
        low = onehot((q_row < 4) & (q_col == 4 * b + q_row))
        high = onehot((q_row >= 4) & (q_col == 4 * b + q_row - 4))
        tiles = [
            dot(low, qry[:, 256 * i : 256 * i + 128]) + dot(high, qry[:, 256 * i + 128 : 256 * i + 256]) for i in range(16)
        ]
        scol[8] = jnp.concatenate(tiles, axis=0).astype(BF16)
        lane = iota((128, 512), 0)
        col = iota((128, 512), 1)
        for j in range(16):
            perm[pl.ds(128 * j, 128), :] = onehot(col == ((lane // 4) % 8) * 64 + j * 4 + lane % 4)
        load_l.wait()
        load_a.wait()
        load_g.wait()

    acc[...] = jnp.zeros_like(acc)

    sel_r = iota((256, 128), 0)
    sel_c = iota((256, 128), 1)

    def prepare(lo, hi):
        def body(part, carry):
            zl = part // 4
            xx = part % 4
            for hh in range(2):
                for cc in range(2):
                    i0 = zl * 16 + xx * 4 + hh * 2 + cc
                    ta = jnp.minimum((76 * i0) // 128, 17)
                    oa = 76 * i0 - 128 * ta
                    tg = jnp.minimum((28 * i0) // 128, 5)
                    og = 28 * i0 - 128 * tg
                    sel_a = onehot((sel_r == sel_c + oa) & (sel_c < 76))
                    sel_g = onehot((sel_r == sel_c - 76 + og) & (sel_c >= 76) & (sel_c < 104))
                    a4 = jnp.concatenate(
                        [av[:, pl.ds(pl.multiple_of((ta + 19 * n) * 128, 128), 256)] for n in range(4)], axis=0
                    )
                    g4 = jnp.concatenate(
                        [gv[:, pl.ds(pl.multiple_of((tg + 7 * n) * 128, 128), 256)] for n in range(4)], axis=0
                    )
                    xa = dot(a4, sel_a).astype(BF16)
                    xg = dot(g4, sel_g).astype(BF16)
                    for n in range(4):
                        xs[cc, 2 * n + zl, xx, 0:128, 128 * hh : 128 * hh + 128] = xa[128 * n : 128 * n + 128]
                        xs[cc, 2 * n + zl, xx, 128:256, 128 * hh : 128 * hh + 128] = xg[128 * n : 128 * n + 128]
            return carry

        lax.fori_loop(lo, hi, body, 0)

    def multiply_a(zz, x0, count):
        for i in range(count):
            w = jnp.concatenate([wa[zz, x0 + i, 0], wa[zz, x0 + i, 1]], axis=1)
            acc[...] += dot_nt(xs[0, zz, x0 + i], w)

    def multiply_b(xx):
        def body(i, carry):
            for zz in (2 * i, 2 * i + 1):
                w = jnp.concatenate([wb[xx, 0, zz], wb[xx, 1, zz]], axis=1)
                acc[...] += dot_nt(xs[1, zz, xx], w)
            return carry

        lax.fori_loop(0, 4, body, 0)

    pl.semaphore_wait(barrier, 18)
    hand_a = {("r", 0, 0): take(), ("r", 0, 1): take()}
    pass_a = {}
    for s in range(1, 5):
        for kind, q in (("r", 0), ("l", 0), ("r", 1), ("l", 1)):
            if s < 4 or (kind, q) in (("r", 0), ("l", 1)):
                hand_a[(kind, s, q)] = take()
                pass_a[(kind, s, q)] = take()
    hand_b = {(n, q): take() for n in ("own", "left", "right", "far") for q in range(2)}
    pass_b = {n: take() for n in ("r0", "r1", "l0", "l1", "far0", "far1")}
    first = [take() for _ in range(15)]

    def place(kind, s):
        return (z + 8 - s) % 8 if kind == "r" else (z + s) % 8

    def slot_a(zz, q):
        return wa.at[zz, pl.ds(2 * q, 2)]

    far = (x + 2) % 4
    place_b = {"own": x, "left": (x + 3) % 4, "right": (x + 1) % 4, "far": far}
    other = {"dp": c_peer}

    @pl.when(c == 0)
    def _():
        base = len(sent)
        ref = wa.at[z, x, h]
        for i, peer in enumerate([h_peer] + x_peers):
            send(ref, ref, first[i], {"dp": peer})
        tables()
        for d in range(3):
            ref = wa.at[z, (x + 3 - d) % 4, h]
            arrived(ref, first[1 + d])
            send(ref, ref, first[4 + d], {"dp": h_peer})
        prepare(0, 2)
        arrived(wa.at[z, x, 1 - h], first[0])
        for d in range(3):
            arrived(wa.at[z, (x + 3 - d) % 4, 1 - h], first[4 + d])
        right = {"dp": at((z + 1) % 8, x, h, c)}
        left = {"dp": at((z + 7) % 8, x, h, c)}

        def pass_on(kind, s, q):
            ref = slot_a(place(kind, s - 1), q)
            send(ref, ref, pass_a[(kind, s, q)], right if kind == "r" else left)

        def hand(kind, s, q):
            ref = slot_a(place(kind, s), q)
            send(ref, ref, hand_a[(kind, s, q)], other)

        for kind, q in (("r", 0), ("l", 1), ("r", 1), ("l", 0)):
            pass_on(kind, 1, q)
        hand("r", 0, 0)
        hand("r", 0, 1)
        prepare(2, 8)
        todo = [(z, 0), (z, 1)]
        for s in range(1, 5):
            ready = []
            for kind, q in (("r", 0), ("l", 1), ("r", 1), ("l", 0)):
                if (kind, s, q) not in pass_a:
                    continue
                arrived(slot_a(place(kind, s), q), pass_a[(kind, s, q)])
                if (kind, s + 1, q) in pass_a:
                    pass_on(kind, s + 1, q)
                hand(kind, s, q)
                ready.append((place(kind, s), q))
            for zz, q in todo:
                multiply_a(zz, 2 * q, 2)
            todo = ready
        for zz, q in todo:
            multiply_a(zz, 2 * q, 2)
        for n in ("own", "left", "right", "far"):
            for q in range(2):
                arrived(wb.at[place_b[n], q], hand_b[(n, q)])
            multiply_b(place_b[n])
        for copy in sent[base:]:
            copy.wait_send()
        del sent[base:]

    @pl.when(c == 1)
    def _():
        base = len(sent)
        ref = wb.at[x, h, z]
        for i, peer in enumerate([h_peer] + z_peers):
            send(ref, ref, first[i], {"dp": peer})
        tables()
        for d in (0, 6, 1, 5, 2, 4, 3):
            ref = wb.at[x, h, (z + 7 - d) % 8]
            arrived(ref, first[1 + d])
            send(ref, ref, first[8 + d], {"dp": h_peer})
        prepare(0, 3)
        arrived(wb.at[x, 1 - h, z], first[0])
        for d in range(7):
            arrived(wb.at[x, 1 - h, (z + 7 - d) % 8], first[8 + d])
        right = {"dp": x_peers[0]}
        left = {"dp": x_peers[2]}
        for name, q, target in (("r0", 0, right), ("l1", 1, left), ("r1", 1, right), ("l0", 0, left)):
            send(wb.at[x, q], wb.at[x, q], pass_b[name], target)
        for q in range(2):
            send(wb.at[x, q], wb.at[x, q], hand_b[("own", q)], other)
        prepare(3, 8)
        xl, xr = place_b["left"], place_b["right"]
        arrived(wb.at[xl, 0], pass_b["r0"])
        send(wb.at[xl, 0], wb.at[xl, 0], pass_b["far0"], right)
        send(wb.at[xl, 0], wb.at[xl, 0], hand_b[("left", 0)], other)
        arrived(wb.at[xr, 1], pass_b["l1"])
        send(wb.at[xr, 1], wb.at[xr, 1], pass_b["far1"], left)
        send(wb.at[xr, 1], wb.at[xr, 1], hand_b[("right", 1)], other)
        multiply_b(x)
        arrived(wb.at[xl, 1], pass_b["r1"])
        send(wb.at[xl, 1], wb.at[xl, 1], hand_b[("left", 1)], other)
        arrived(wb.at[xr, 0], pass_b["l0"])
        send(wb.at[xr, 0], wb.at[xr, 0], hand_b[("right", 0)], other)
        multiply_b(xl)
        arrived(wb.at[far, 0], pass_b["far0"])
        send(wb.at[far, 0], wb.at[far, 0], hand_b[("far", 0)], other)
        arrived(wb.at[far, 1], pass_b["far1"])
        send(wb.at[far, 1], wb.at[far, 1], hand_b[("far", 1)], other)
        multiply_b(xr)
        multiply_b(far)
        for s in range(5):
            for kind, q in (("r", 0), ("l", 1), ("r", 1), ("l", 0)):
                if (kind, s, q) not in hand_a:
                    continue
                arrived(slot_a(place(kind, s), q), hand_a[(kind, s, q)])
                multiply_a(place(kind, s), 2 * q, 2)
        for copy in sent[base:]:
            copy.wait_send()
        del sent[base:]

    tok = iota((128, 64), 0)
    length = jnp.zeros((128, 64), jnp.int32)
    for p in range(4):
        length = jnp.where(tok // 32 == p, lens[0, p], length)
    mask = jnp.where(tok % 32 < length, 1.0, 0.0).astype(F32)
    right_proj = acc[0:128].astype(BF16)
    left_proj = (mask * acc[128:256]).astype(BF16)
    row = iota((128, 128), 0)
    colm = iota((128, 128), 1)
    mine = jnp.where(colm // 32 == row % 4, 1.0, 0.0).astype(F32)
    k_row = iota((128, 64), 0)
    k_col = iota((128, 64), 1)
    j_row = iota((64, 128), 0)
    j_col = iota((64, 128), 1)
    total = jnp.zeros((128, 128), F32)
    for par in range(2):
        spread = dot_nt(onehot(k_col == 2 * (k_row // 4) + par), left_proj)
        lefts = (spread * mine).astype(BF16)
        rights = dot(right_proj, onehot(j_col == j_row + 64 * par)).astype(BF16)
        total = total + dot(lefts, rights)
    sketch = total.astype(BF16)
    for m in range(32):
        sk[:, 128 * m : 128 * m + 128] = total[4 * m : 4 * m + 4].astype(BF16)
    srow[c, x, h] = sketch
    scol[z] = sketch

    s_h = take()
    send(srow.at[c, x, h], srow.at[c, x, h], s_h, {"dp": h_peer})
    s_z = [take() for _ in range(7)]
    for d in range(7):
        send(scol.at[z], scol.at[z], s_z[d], {"dp": z_peers[d]})
    arrived(srow.at[c, x, 1 - h], s_h)
    s_x = [take() for _ in range(3)]
    s_c = [take() for _ in range(4)]
    for d in range(3):
        send(srow.at[c, x], srow.at[c, x], s_x[d], {"dp": x_peers[d]})
    send(srow.at[c, x], srow.at[c, x], s_c[0], {"dp": c_peer})
    for d in range(3):
        xx = (x + 3 - d) % 4
        arrived(srow.at[c, xx], s_x[d])
        send(srow.at[c, xx], srow.at[c, xx], s_c[d + 1], {"dp": c_peer})
    for d in range(7):
        arrived(scol.at[(z + 7 - d) % 8], s_z[d])
    for d in range(4):
        arrived(srow.at[1 - c, (x + 4 - d) % 4], s_c[d])

    squares = jnp.zeros((8, 128), F32)
    for cc in range(2):
        for xx in range(4):
            v = srow[cc, xx].astype(F32)
            squares = squares + jnp.sum((v * v).reshape(32, 8, 128), axis=0)
    tz[z] = squares
    t_z = [take() for _ in range(7)]
    for d in range(7):
        send(tz.at[z], tz.at[z], t_z[d], {"dp": z_peers[d]})
    gram = jnp.zeros((256, 144), F32)
    for u in range(4):
        rows = [srow[:, :, :, pl.ds(32 * u + 16 * v, 16), :].reshape(256, 128) for v in range(2)]
        cols = [scol[:, pl.ds(32 * u + 16 * v, 16), :].reshape(144, 128) for v in range(2)]
        gram = gram + dot_nt(jnp.concatenate(rows, axis=1), jnp.concatenate(cols, axis=1))
    gr = iota((256, 144), 0)
    gc = iota((256, 144), 1)
    gram = jnp.where((gr // 4) % 4 == (gc // 4) % 4, gram, 0.0)
    pr = iota((64, 256), 0)
    pc = iota((64, 256), 1)
    blk = pc // 16
    pick_rows = onehot(pr == ((blk // 2) % 4) * 16 + (blk % 2) * 8 + (blk // 8) * 4 + pc % 4)
    half = sum(dot(pick_rows, v) for v in pieces(gram))
    nr = iota((144, 256), 0)
    nc = iota((144, 256), 1)
    in_k = (nr < 128) & (nc < 128) & (nc % 32 == (nr // 16) * 4 + nr % 4)
    in_q = (nr >= 128) & (nc >= 128) & ((nc - 128) // 16 == b % 8) & (nc % 4 == nr % 4)
    pick_cols = onehot(in_k | in_q)
    spread = sum(dot(v, pick_cols) for v in pieces(half))
    yr = iota((64, 256), 0)
    yc = iota((64, 256), 1)
    quarter = jnp.where(yc < 128, yc // 32, (yc // 4) % 4) == yr // 16
    spread = jnp.where(quarter, spread, 0.0)
    lx[h, ly] = spread[0:16] + spread[16:32] + spread[32:48] + spread[48:64]

    l_s = [(d, hh, take()) for d in range(4) for hh in range(2) if d + hh > 0]
    for d, hh, sem in l_s:
        peer = {"dp": at(z, x, (h + hh) % 2, c), "layer": (ly + d) % 4}
        send(lx.at[h, ly], lx.at[h, ly], sem, peer)
    for d, hh, sem in l_s:
        arrived(lx.at[(h + hh) % 2, (ly + 4 - d) % 4], sem)
    for hh in range(2):
        kb[c, x, hh] = (lx[hh, 0] + lx[hh, 1]) + (lx[hh, 2] + lx[hh, 3])
    for d in range(7):
        arrived(tz.at[(z + 7 - d) % 8], t_z[d])
    plane_sums = tz[0]
    for n in range(1, 8):
        plane_sums = plane_sums + tz[n]
    tl[ly] = plane_sums
    t_l = [take() for _ in range(3)]
    for d in range(3):
        send(tl.at[ly], tl.at[ly], t_l[d], {"layer": (ly + 1 + d) % 4})
    k_x = [take() for _ in range(3)]
    k_c = [take() for _ in range(4)]
    for d in range(3):
        send(kb.at[c, x], kb.at[c, x], k_x[d], {"dp": x_peers[d]})
    send(kb.at[c, x], kb.at[c, x], k_c[0], {"dp": c_peer})
    for d in range(3):
        xx = (x + 3 - d) % 4
        arrived(kb.at[c, xx], k_x[d])
        send(kb.at[c, xx], kb.at[c, xx], k_c[d + 1], {"dp": c_peer})
    for d in range(4):
        arrived(kb.at[1 - c, (x + 4 - d) % 4], k_c[d])

    def tall(v):
        return jnp.concatenate([v, v, v, v], axis=0)

    r4 = iota((64, 128), 0) // 16
    l4 = iota((64, 128), 1)
    wide = []
    side = [jnp.zeros((16, 128), F32), jnp.zeros((16, 128), F32)]
    for j in range(16):
        v = kb[j % 2, j // 4, (j // 2) % 2]
        wide.append(jnp.where(l4 // 32 == r4, tall(v[:, 0:128]), 0.0))
        side[j // 8] = side[j // 8] + v[:, 128:256]
    flat = jnp.concatenate(wide, axis=1)
    part = sum(dot(v, perm[...]) for v in pieces(flat))
    sides = jnp.concatenate([jnp.where((l4 // 4) % 4 == r4, tall(v), 0.0) for v in side], axis=1)
    ir = iota((256, 128), 0)
    ic = iota((256, 128), 1)
    place_q = onehot(ic == (ir // 16) * 4 + ir % 4)
    part_q = sum(dot(v, place_q) for v in pieces(sides))
    kin[pl.ds(pl.multiple_of(64 * z, 64), 64), 0:512] = part
    kin[pl.ds(pl.multiple_of(64 * z, 64), 64), 512:640] = part_q
    for d in range(3):
        arrived(tl.at[(ly + 3 - d) % 4], t_l[d])
    mean_diag = jnp.sum((tl[0] + tl[1]) + (tl[2] + tl[3])) / 512.0
    damping = damp_ratio * mean_diag
    ring = {}
    for s in range(1, 5):
        for kind, q in (("r", 0), ("l", 1), ("r", 1), ("l", 0)):
            if s < 4 or (kind, q) in (("r", 0), ("l", 1)):
                ring[(kind, s, q)] = (take(), take())
    right = {"dp": at((z + 1) % 8, x, h, c)}
    left = {"dp": at((z + 7) % 8, x, h, c)}

    def rows_at(cc, zz, q):
        return kin.at[pl.ds(pl.multiple_of(64 * zz + 32 * cc + 16 * q, 16), 16)]

    def pass_rows(kind, s, q):
        ref = rows_at(c, place(kind, s - 1), q)
        send(ref, ref, ring[(kind, s, q)][0], right if kind == "r" else left)

    swing = 2 * (z % 2) - 1
    home = z // 2
    order = [home, (home + 4 + swing) % 4, (home + 4 - swing) % 4, (home + 2) % 4]
    spans = [pl.ds(pl.multiple_of(128 * i, 128), 128) for i in order]
    here = iota((128, 640), 0)
    there = iota((128, 640), 1)

    def eliminate(t):
        a[t] = kin[spans[t], :] + jnp.where(there == here + 128 * order[t], damping, 0.0)
        for n in range(t):
            a[t] = a[t] - jnp.dot(a[t, :, spans[n]], a[n], precision=HIGH, preferred_element_type=F32)
        inv = invert(a[t, :, spans[t]], lambda: take_hop(t + 2))
        a[t] = jnp.dot(inv, a[t], precision=HIGH, preferred_element_type=F32)

    for kind, q in (("r", 0), ("l", 1), ("r", 1), ("l", 0)):
        pass_rows(kind, 1, q)
    def take_hop(s):
        for kind, _, q in [n for n in ring if n[1] == s]:
            ref = rows_at(c, place(kind, s), q)
            arrived(ref, ring[(kind, s, q)][0])
            if (kind, s + 1, q) in ring:
                pass_rows(kind, s + 1, q)
            send(ref, ref, ring[(kind, s, q)][1], other)

    take_hop(1)
    for s in range(1, 5):
        for kind, _, q in [n for n in ring if n[1] == s]:
            arrived(rows_at(1 - c, place(kind, s), q), ring[(kind, s, q)][1])
        eliminate(s - 1)

    def apply(left_rows, n, value):
        return jnp.dot(left_rows(spans[n]), value, precision=HIGH, preferred_element_type=F32)

    x3 = a[3, :, 512:640]
    x2 = a[2, :, 512:640] - apply(lambda at_: a[2, :, at_], 3, x3)
    x1 = a[1, :, 512:640] - apply(lambda at_: a[1, :, at_], 3, x3) - apply(lambda at_: a[1, :, at_], 2, x2)
    pick = jnp.where(iota((8, 128), 1) == (me * 4 - 128 * home) + iota((8, 128), 0), 1.0, 0.0).astype(F32)
    own_x = jnp.dot(pick, a[0, :, 512:640], precision=HIGH, preferred_element_type=F32)
    for n, value in ((3, x3), (2, x2), (1, x1)):
        coef = jnp.dot(pick, a[0, :, spans[n]], precision=HIGH, preferred_element_type=F32)
        own_x = own_x - jnp.dot(coef, value, precision=HIGH, preferred_element_type=F32)
    own_x = own_x[0:4]
    load_x.wait()
    lanes = iota((4, 128), 1)
    spot = iota((4, 8), 1)
    out = jnp.zeros((4, 8), F32)
    for n in range(8):
        chosen = jnp.sum(jnp.where(lanes == qidx[:, n : n + 1], own_x, 0.0), axis=1, keepdims=True)
        out = jnp.where(spot == n, chosen, out)
    scores[...] = jnp.sqrt(mean_diag) * out
    for copy in sent:
        copy.wait_send()


def run_front(act, grd, inb, outb, qry, lens, qidx):
    vmem = pl.BlockSpec(memory_space=pltpu.VMEM)
    hbm = pl.BlockSpec(memory_space=pltpu.HBM)
    return pl.pallas_call(
        front,
        out_shape=(jax.ShapeDtypeStruct((4, 4096), BF16), jax.ShapeDtypeStruct((4, 8), F32)),
        in_specs=[hbm] * 7,
        out_specs=(vmem, vmem),
        scratch_shapes=[
            pltpu.VMEM((512, 640), F32),
            pltpu.VMEM((4, 128, 640), F32),
            pltpu.VMEM((8, 8, 128), F32),
            pltpu.VMEM((4, 8, 128), F32),
            pltpu.VMEM((4, 8), jnp.int32),
            pltpu.VMEM(act.shape, BF16),
            pltpu.VMEM(grd.shape, BF16),
            pltpu.VMEM(inb.shape, BF16),
            pltpu.VMEM(outb.shape, BF16),
            pltpu.VMEM(qry.shape, BF16),
            pltpu.SMEM((1, 4), jnp.int32),
            pltpu.VMEM((2, 8, 4, 256, 256), BF16),
            pltpu.VMEM((8, 4, 2, 64, 128), BF16),
            pltpu.VMEM((4, 2, 8, 64, 128), BF16),
            pltpu.VMEM((2, 4, 2, 128, 128), BF16),
            pltpu.VMEM((9, 128, 128), BF16),
            pltpu.VMEM((2, 4, 16, 256), F32),
            pltpu.VMEM((2, 4, 2, 16, 256), F32),
            pltpu.VMEM((2048, 512), BF16),
            pltpu.VMEM((256, 64), F32),
            pltpu.SemaphoreType.DMA((7,)),
            pltpu.SemaphoreType.DMA((SEMS,)),
            pltpu.SemaphoreType.DMA((SEMS,)),
        ],
        compiler_params=pltpu.CompilerParams(collective_id=0, has_side_effects=True, vmem_limit_bytes=48 * 1024 * 1024),
        name="front",
    )(*[pltpu.with_memory_space_constraint(v, pltpu.HBM) for v in (act, grd, inb, outb, qry, lens, qidx)])


def local(activations, out_grads, in_basis, out_basis, queries, pair_lengths, query_index):
    sketch, scores = run_front(
        activations[0], out_grads[0], in_basis[0].T, out_basis[0], queries[0], pair_lengths, query_index
    )
    return sketch[None], scores


def solution(mesh):
    placed = (
        P("layer", "dp", None),
        P("layer", "dp", None),
        P("layer", "dp", None),
        P("layer", "dp", None),
        P("layer", None, None),
        P("dp", None),
        P("dp", None),
    )
    return jax.shard_map(
        local,
        mesh=mesh,
        in_specs=placed,
        out_specs=(P("layer", "dp", None), P("dp", None)),
        check_vma=False,
    )
```

```python
import jax
import jax.numpy as jnp
from jax import lax
from jax.experimental import pallas as pl
from jax.experimental.pallas import tpu as pltpu
from jax.sharding import PartitionSpec as P

MESH = pl.DeviceIdType.MESH
damp_ratio = 0.5
F32 = jnp.float32
BF16 = jnp.bfloat16
NT = (((1,), (1,)), ((), ()))
SEMS = 192


def iota(shape, dim):
    return lax.broadcasted_iota(jnp.int32, shape, dim)


def onehot(cond):
    return jnp.where(cond, 1.0, 0.0).astype(BF16)


def pieces(v):
    hi = v.astype(BF16)
    rest = v - hi.astype(F32)
    mid = rest.astype(BF16)
    return hi, mid, (rest - mid.astype(F32)).astype(BF16)


def dot(a, b):
    return jnp.dot(a, b, preferred_element_type=F32)


def dot_nt(a, b):
    return lax.dot_general(a, b, NT, preferred_element_type=F32)


HIGH = lax.Precision.HIGHEST


STRIP = 64
PANEL = 16
PV = 2


def invert(d, between):
    sub = iota((8, 128), 0)
    lane = iota((8, 128), 1)
    big_row = iota((STRIP, 128), 0)
    big_col = iota((STRIP, 128), 1) // STRIP
    per = STRIP // 8
    count = 128 // STRIP
    strips = [d[STRIP * s : STRIP * s + STRIP, :] for s in range(count)]
    for s in range(count):
        rows = [strips[s][8 * i : 8 * i + 8, :] for i in range(per)]
        for p in range(0, per, PV):
            first = s * STRIP + 8 * p
            inside = lane // PANEL == first // PANEL
            heads = rows[p : p + PV]
            cols = [[jnp.broadcast_to(v[:, first + k : first + k + 1], (8, 128)) for v in heads] for k in range(PANEL)]
            heads = [
                jnp.where(inside, jnp.where(lane % PANEL == sub + 8 * n, 1.0, 0.0), v) for n, v in enumerate(heads)
            ]
            for k in range(PANEL):
                n0, r0 = k // 8, k % 8
                here = sub == r0
                f = cols[k]
                pivot = 1.0 / f[n0][r0 : r0 + 1, :]
                for j in range(k + 1, PANEL):
                    g = cols[j][n0][r0 : r0 + 1, :] * pivot
                    cols[j] = [
                        jnp.where(here, g, v - f[n] * g) if n == n0 else v - f[n] * g for n, v in enumerate(cols[j])
                    ]
                lead = heads[n0][r0 : r0 + 1, :] * pivot
                heads = [
                    jnp.where(here, lead, v - f[n] * lead) if n == n0 else v - f[n] * lead for n, v in enumerate(heads)
                ]
            rows[p : p + PV] = heads
            others = [i for i in range(per) if not p <= i < p + PV]
            if others:
                leads = [jnp.broadcast_to(heads[k // 8][k % 8 : k % 8 + 1, :], (8, 128)) for k in range(PANEL)]
                for i in others:
                    v = rows[i]
                    r = jnp.where(inside, 0.0, v)
                    for k in range(PANEL):
                        r = r - v[:, first + k : first + k + 1] * leads[k]
                    rows[i] = r
        done = jnp.concatenate(rows, axis=0) if per > 1 else rows[0]
        zero = jnp.zeros((STRIP, 128), F32)
        placed = jnp.concatenate([done if t == s else zero for t in range(count)], axis=0)
        new = [None] * count
        new[s] = done
        for t in [(s + i) % count for i in range(1, count)]:
            v = strips[t]
            side = jnp.where(big_col == s, v, 0.0)
            keep = jnp.where(big_col == s, 0.0, v)
            new[t] = keep - jnp.dot(side, placed, precision=HIGH, preferred_element_type=F32)
        strips = new
        if s == 0:
            between()
    return jnp.concatenate(strips, axis=0)


def front(act, grd, inb_hbm, outb_hbm, qry_hbm, lens_hbm, qidx_hbm, sk, scores, kin, a, tz, tl, qidx, av, gv, inb, outb, qry, lens, xs, wa, wb, srow, scol, lx, kb, perm, acc, in_sem, ssem, rsem):
    me = lax.axis_index("dp")
    ly = lax.axis_index("layer")
    c = me % 2
    h = (me // 2) % 2
    x = (me // 4) % 4
    z = me // 16
    b = me % 16

    def at(zz, xx, hh, cc):
        return ((zz * 4 + xx) * 2 + hh) * 2 + cc

    h_peer = at(z, x, 1 - h, c)
    c_peer = at(z, x, h, 1 - c)
    x_peers = [at(z, (x + d) % 4, h, c) for d in range(1, 4)]
    z_peers = [at((z + d) % 8, x, h, c) for d in range(1, 8)]

    load_a = pltpu.make_async_copy(act, av, in_sem.at[0])
    load_g = pltpu.make_async_copy(grd, gv, in_sem.at[1])
    load_l = pltpu.make_async_copy(lens_hbm, lens, in_sem.at[2])
    load_i = pltpu.make_async_copy(inb_hbm, inb, in_sem.at[3])
    load_o = pltpu.make_async_copy(outb_hbm, outb, in_sem.at[4])
    load_q = pltpu.make_async_copy(qry_hbm, qry, in_sem.at[5])
    load_x = pltpu.make_async_copy(qidx_hbm, qidx, in_sem.at[6])
    for load in (load_i, load_o, load_a, load_g, load_q, load_l, load_x):
        load.start()

    barrier = pltpu.get_barrier_semaphore()
    for peer in [h_peer, c_peer] + x_peers + z_peers:
        pl.semaphore_signal(barrier, inc=1, device_id={"dp": peer}, device_id_type=MESH)
    for d in range(1, 4):
        for hh in range(2):
            peer = {"dp": at(z, x, (h + hh) % 2, c), "layer": (ly + d) % 4}
            pl.semaphore_signal(barrier, inc=1, device_id=peer, device_id_type=MESH)

    used = [0]
    sent = []

    def take():
        used[0] += 1
        return used[0] - 1

    def send(src, dst, sem, device):
        copy = pltpu.make_async_remote_copy(
            src_ref=src, dst_ref=dst, send_sem=ssem.at[sem], recv_sem=rsem.at[sem], device_id=device, device_id_type=MESH
        )
        copy.start()
        sent.append(copy)

    def arrived(slot, sem):
        pltpu.make_async_remote_copy(
            src_ref=slot, dst_ref=slot, send_sem=ssem.at[sem], recv_sem=rsem.at[sem], device_id={"dp": c_peer}, device_id_type=MESH
        ).wait_recv()

    eye = onehot(iota((64, 64), 0) == iota((64, 64), 1))
    load_i.wait()
    load_o.wait()
    out_t = dot_nt(eye, outb[...]).astype(BF16)
    in_at = onehot(iota((76, 128), 0) == iota((76, 128), 1))
    out_at = onehot(iota((28, 128), 0) + 76 == iota((28, 128), 1))
    own = (dot(inb[...], in_at) + dot(out_t, out_at)).astype(BF16)

    @pl.when(c == 0)
    def _():
        wa[z, h, x] = own

    @pl.when(c == 1)
    def _():
        wb[x, h, z] = own

    def tables():
        load_q.wait()
        q_row = iota((8, 64), 0)
        q_col = iota((8, 64), 1)
        low = onehot((q_row < 4) & (q_col == 4 * b + q_row))
        high = onehot((q_row >= 4) & (q_col == 4 * b + q_row - 4))
        tiles = [
            dot(low, qry[:, 256 * i : 256 * i + 128]) + dot(high, qry[:, 256 * i + 128 : 256 * i + 256]) for i in range(16)
        ]
        scol[8] = jnp.concatenate(tiles, axis=0).astype(BF16)
        lane = iota((128, 512), 0)
        col = iota((128, 512), 1)
        for j in range(16):
            perm[pl.ds(128 * j, 128), :] = onehot(col == ((lane // 4) % 8) * 64 + j * 4 + lane % 4)
        load_l.wait()
        load_x.wait()
        load_a.wait()
        load_g.wait()

    acc[...] = jnp.zeros_like(acc)

    sel_r = iota((256, 128), 0)
    sel_c = iota((256, 128), 1)

    def prepare(lo, hi):
        def body(part, carry):
            zl = part // 4
            xx = part % 4
            for hh in range(2):
                for cc in range(2):
                    i0 = zl * 16 + xx * 4 + hh * 2 + cc
                    ta = jnp.minimum((76 * i0) // 128, 17)
                    oa = 76 * i0 - 128 * ta
                    tg = jnp.minimum((28 * i0) // 128, 5)
                    og = 28 * i0 - 128 * tg
                    sel_a = onehot((sel_r == sel_c + oa) & (sel_c < 76))
                    sel_g = onehot((sel_r == sel_c - 76 + og) & (sel_c >= 76) & (sel_c < 104))
                    a4 = jnp.concatenate(
                        [av[:, pl.ds(pl.multiple_of((ta + 19 * n) * 128, 128), 256)] for n in range(4)], axis=0
                    )
                    g4 = jnp.concatenate(
                        [gv[:, pl.ds(pl.multiple_of((tg + 7 * n) * 128, 128), 256)] for n in range(4)], axis=0
                    )
                    xa = dot(a4, sel_a).astype(BF16)
                    xg = dot(g4, sel_g).astype(BF16)
                    for n in range(4):
                        xs[cc, 2 * n + zl, xx, 0:128, 128 * hh : 128 * hh + 128] = xa[128 * n : 128 * n + 128]
                        xs[cc, 2 * n + zl, xx, 128:256, 128 * hh : 128 * hh + 128] = xg[128 * n : 128 * n + 128]
            return carry

        lax.fori_loop(lo, hi, body, 0)

    def multiply_a(zz):
        for i in range(4):
            w = jnp.concatenate([wa[zz, 0, i], wa[zz, 1, i]], axis=1)
            acc[...] += dot_nt(xs[0, zz, i], w)

    def multiply_b(xx):
        def body(i, carry):
            for zz in (2 * i, 2 * i + 1):
                w = jnp.concatenate([wb[xx, 0, zz], wb[xx, 1, zz]], axis=1)
                acc[...] += dot_nt(xs[1, zz, xx], w)
            return carry

        lax.fori_loop(0, 4, body, 0)

    pl.semaphore_wait(barrier, 18)
    hand_a = {("r", 0, 0): take(), ("r", 0, 1): take()}
    pass_a = {}
    for s in range(1, 5):
        for kind, q in (("r", 0), ("l", 0), ("r", 1), ("l", 1)):
            if s < 4 or (kind, q) in (("r", 0), ("l", 1)):
                hand_a[(kind, s, q)] = take()
                pass_a[(kind, s, q)] = take()
    hand_b = {(n, q): take() for n in ("own", "left", "right", "far") for q in range(2)}
    pass_b = {n: take() for n in ("r0", "r1", "l0", "l1", "far0", "far1")}
    first = [take() for _ in range(15)]

    def place(kind, s):
        return (z + 8 - s) % 8 if kind == "r" else (z + s) % 8

    def slot_a(zz, q):
        return wa.at[zz, (h + q) % 2]

    far = (x + 2) % 4
    place_b = {"own": x, "left": (x + 3) % 4, "right": (x + 1) % 4, "far": far}
    other = {"dp": c_peer}

    @pl.when(c == 0)
    def _():
        base = len(sent)
        ref = wa.at[z, h, x]
        for i, peer in enumerate([h_peer] + x_peers):
            send(ref, ref, first[i], {"dp": peer})
        tables()
        right = {"dp": at((z + 1) % 8, x, h, c)}
        left = {"dp": at((z + 7) % 8, x, h, c)}

        def pass_on(kind, s, q):
            ref = slot_a(place(kind, s - 1), q)
            send(ref, ref, pass_a[(kind, s, q)], right if kind == "r" else left)

        def hand(kind, s, q):
            ref = slot_a(place(kind, s), q)
            send(ref, ref, hand_a[(kind, s, q)], other)

        def hop(s, q):
            for kind in ("r", "l"):
                if (kind, s, q) in pass_a:
                    arrived(slot_a(place(kind, s), q), pass_a[(kind, s, q)])
                    if (kind, s + 1, q) in pass_a:
                        pass_on(kind, s + 1, q)
                    hand(kind, s, q)

        def theirs(name):
            for q in range(2):
                arrived(wb.at[place_b[name], (h + q) % 2], hand_b[(name, q)])
            multiply_b(place_b[name])

        for d in range(3):
            ref = wa.at[z, h, (x + 3 - d) % 4]
            arrived(ref, first[1 + d])
            send(ref, ref, first[4 + d], {"dp": h_peer})
        pass_on("r", 1, 0)
        pass_on("l", 1, 0)
        hand("r", 0, 0)
        prepare(0, 3)
        hop(1, 0)
        arrived(wa.at[z, 1 - h, x], first[0])
        for d in range(3):
            arrived(wa.at[z, 1 - h, (x + 3 - d) % 4], first[4 + d])
        pass_on("r", 1, 1)
        pass_on("l", 1, 1)
        hand("r", 0, 1)
        prepare(3, 5)
        hop(2, 0)
        prepare(5, 7)
        hop(1, 1)
        prepare(7, 8)
        hop(3, 0)
        multiply_a(z)
        hop(2, 1)
        multiply_a(place("r", 1))
        multiply_a(place("l", 1))
        theirs("own")
        hop(4, 0)
        hop(3, 1)
        multiply_a(place("r", 2))
        multiply_a(place("l", 2))
        theirs("left")
        theirs("right")
        hop(4, 1)
        multiply_a(place("r", 3))
        multiply_a(place("l", 3))
        theirs("far")
        multiply_a(place("r", 4))
        for copy in sent[base:]:
            copy.wait_send()
        del sent[base:]

    @pl.when(c == 1)
    def _():
        base = len(sent)
        ref = wb.at[x, h, z]
        for i, peer in enumerate([h_peer] + z_peers):
            send(ref, ref, first[i], {"dp": peer})
        tables()
        for d in (0, 6, 1, 5, 2, 4, 3):
            ref = wb.at[x, h, (z + 7 - d) % 8]
            arrived(ref, first[1 + d])
            send(ref, ref, first[8 + d], {"dp": h_peer})
        right = {"dp": x_peers[0]}
        left = {"dp": x_peers[2]}
        xl, xr = place_b["left"], place_b["right"]

        def slot_b(xx, q):
            return wb.at[xx, (h + q) % 2]

        def spread_own(q):
            send(slot_b(x, q), slot_b(x, q), pass_b["r" + str(q)], right)
            send(slot_b(x, q), slot_b(x, q), pass_b["l" + str(q)], left)
            send(slot_b(x, q), slot_b(x, q), hand_b[("own", q)], other)

        def got_b(xx, q, name, to, sem, target):
            arrived(slot_b(xx, q), pass_b[name])
            if target is not None:
                send(slot_b(xx, q), slot_b(xx, q), pass_b[sem], target)
            send(slot_b(xx, q), slot_b(xx, q), hand_b[(to, q)], other)

        spread_own(0)
        prepare(0, 2)
        got_b(xl, 0, "r0", "left", "far0", right)
        got_b(xr, 0, "l0", "right", None, None)
        prepare(2, 3)
        arrived(wb.at[x, 1 - h, z], first[0])
        for d in range(7):
            arrived(wb.at[x, 1 - h, (z + 7 - d) % 8], first[8 + d])
        spread_own(1)
        got_b(far, 0, "far0", "far", None, None)
        prepare(3, 8)
        got_b(xr, 1, "l1", "right", "far1", left)
        got_b(xl, 1, "r1", "left", None, None)
        multiply_b(x)
        multiply_b(xl)
        multiply_b(xr)
        got_b(far, 1, "far1", "far", None, None)
        multiply_b(far)
        for s in range(5):
            for kind, q in (("r", 0), ("l", 0), ("r", 1), ("l", 1)):
                if (kind, s, q) in hand_a:
                    arrived(slot_a(place(kind, s), q), hand_a[(kind, s, q)])
            multiply_a(place("r", s))
            if 0 < s < 4:
                multiply_a(place("l", s))
        for copy in sent[base:]:
            copy.wait_send()
        del sent[base:]

    tok = iota((128, 64), 0)
    length = jnp.zeros((128, 64), jnp.int32)
    for p in range(4):
        length = jnp.where(tok // 32 == p, lens[0, p], length)
    mask = jnp.where(tok % 32 < length, 1.0, 0.0).astype(F32)
    right_proj = acc[0:128].astype(BF16)
    left_proj = (mask * acc[128:256]).astype(BF16)
    row = iota((128, 128), 0)
    colm = iota((128, 128), 1)
    mine = jnp.where(colm // 32 == row % 4, 1.0, 0.0).astype(F32)
    k_row = iota((128, 64), 0)
    k_col = iota((128, 64), 1)
    j_row = iota((64, 128), 0)
    j_col = iota((64, 128), 1)
    total = jnp.zeros((128, 128), F32)
    for par in range(2):
        spread = dot_nt(onehot(k_col == 2 * (k_row // 4) + par), left_proj)
        lefts = (spread * mine).astype(BF16)
        rights = dot(right_proj, onehot(j_col == j_row + 64 * par)).astype(BF16)
        total = total + dot(lefts, rights)
    sketch = total.astype(BF16)
    for m in range(32):
        sk[:, 128 * m : 128 * m + 128] = total[4 * m : 4 * m + 4].astype(BF16)
    srow[c, x, h] = sketch
    scol[z] = sketch

    s_h = take()
    send(srow.at[c, x, h], srow.at[c, x, h], s_h, {"dp": h_peer})
    s_z = [take() for _ in range(7)]
    for d in range(7):
        send(scol.at[z], scol.at[z], s_z[d], {"dp": z_peers[d]})
    arrived(srow.at[c, x, 1 - h], s_h)
    s_x = [take() for _ in range(3)]
    s_c = [take() for _ in range(4)]
    for d in range(3):
        send(srow.at[c, x], srow.at[c, x], s_x[d], {"dp": x_peers[d]})
    send(srow.at[c, x], srow.at[c, x], s_c[0], {"dp": c_peer})
    for d in range(3):
        xx = (x + 3 - d) % 4
        arrived(srow.at[c, xx], s_x[d])
        send(srow.at[c, xx], srow.at[c, xx], s_c[d + 1], {"dp": c_peer})
    for d in range(7):
        arrived(scol.at[(z + 7 - d) % 8], s_z[d])
    for d in range(4):
        arrived(srow.at[1 - c, (x + 4 - d) % 4], s_c[d])

    squares = jnp.zeros((8, 128), F32)
    for cc in range(2):
        for xx in range(4):
            v = srow[cc, xx].astype(F32)
            squares = squares + jnp.sum((v * v).reshape(32, 8, 128), axis=0)
    tz[z] = squares
    t_z = [take() for _ in range(7)]
    for d in range(7):
        send(tz.at[z], tz.at[z], t_z[d], {"dp": z_peers[d]})
    gram = jnp.zeros((256, 144), F32)
    for u in range(4):
        rows = [srow[:, :, :, pl.ds(32 * u + 16 * v, 16), :].reshape(256, 128) for v in range(2)]
        cols = [scol[:, pl.ds(32 * u + 16 * v, 16), :].reshape(144, 128) for v in range(2)]
        gram = gram + dot_nt(jnp.concatenate(rows, axis=1), jnp.concatenate(cols, axis=1))
    gr = iota((256, 144), 0)
    gc = iota((256, 144), 1)
    gram = jnp.where((gr // 4) % 4 == (gc // 4) % 4, gram, 0.0)
    pr = iota((64, 256), 0)
    pc = iota((64, 256), 1)
    blk = pc // 16
    pick_rows = onehot(pr == ((blk // 2) % 4) * 16 + (blk % 2) * 8 + (blk // 8) * 4 + pc % 4)
    half = sum(dot(pick_rows, v) for v in pieces(gram))
    nr = iota((144, 256), 0)
    nc = iota((144, 256), 1)
    in_k = (nr < 128) & (nc < 128) & (nc % 32 == (nr // 16) * 4 + nr % 4)
    in_q = (nr >= 128) & (nc >= 128) & ((nc - 128) // 16 == b % 8) & (nc % 4 == nr % 4)
    pick_cols = onehot(in_k | in_q)
    spread = sum(dot(v, pick_cols) for v in pieces(half))
    yr = iota((64, 256), 0)
    yc = iota((64, 256), 1)
    quarter = jnp.where(yc < 128, yc // 32, (yc // 4) % 4) == yr // 16
    spread = jnp.where(quarter, spread, 0.0)
    lx[h, ly] = spread[0:16] + spread[16:32] + spread[32:48] + spread[48:64]

    l_s = [(d, hh, take()) for d in range(4) for hh in range(2) if d + hh > 0]
    for d, hh, sem in l_s:
        peer = {"dp": at(z, x, (h + hh) % 2, c), "layer": (ly + d) % 4}
        send(lx.at[h, ly], lx.at[h, ly], sem, peer)
    for d, hh, sem in l_s:
        arrived(lx.at[(h + hh) % 2, (ly + 4 - d) % 4], sem)
    for hh in range(2):
        kb[c, x, hh] = (lx[hh, 0] + lx[hh, 1]) + (lx[hh, 2] + lx[hh, 3])
    for d in range(7):
        arrived(tz.at[(z + 7 - d) % 8], t_z[d])
    plane_sums = tz[0]
    for n in range(1, 8):
        plane_sums = plane_sums + tz[n]
    tl[ly] = plane_sums
    t_l = [take() for _ in range(3)]
    for d in range(3):
        send(tl.at[ly], tl.at[ly], t_l[d], {"layer": (ly + 1 + d) % 4})
    k_x = [take() for _ in range(3)]
    k_c = [take() for _ in range(4)]
    for d in range(3):
        send(kb.at[c, x], kb.at[c, x], k_x[d], {"dp": x_peers[d]})
    send(kb.at[c, x], kb.at[c, x], k_c[0], {"dp": c_peer})
    for d in range(3):
        xx = (x + 3 - d) % 4
        arrived(kb.at[c, xx], k_x[d])
        send(kb.at[c, xx], kb.at[c, xx], k_c[d + 1], {"dp": c_peer})
    for d in range(4):
        arrived(kb.at[1 - c, (x + 4 - d) % 4], k_c[d])

    def tall(v):
        return jnp.concatenate([v, v, v, v], axis=0)

    r4 = iota((64, 128), 0) // 16
    l4 = iota((64, 128), 1)
    wide = []
    side = [jnp.zeros((16, 128), F32), jnp.zeros((16, 128), F32)]
    for j in range(16):
        v = kb[j % 2, j // 4, (j // 2) % 2]
        wide.append(jnp.where(l4 // 32 == r4, tall(v[:, 0:128]), 0.0))
        side[j // 8] = side[j // 8] + v[:, 128:256]
    flat = jnp.concatenate(wide, axis=1)
    part = sum(dot(v, perm[...]) for v in pieces(flat))
    sides = jnp.concatenate([jnp.where((l4 // 4) % 4 == r4, tall(v), 0.0) for v in side], axis=1)
    ir = iota((256, 128), 0)
    ic = iota((256, 128), 1)
    place_q = onehot(ic == (ir // 16) * 4 + ir % 4)
    part_q = sum(dot(v, place_q) for v in pieces(sides))
    kin[pl.ds(pl.multiple_of(64 * z, 64), 64), 0:512] = part
    kin[pl.ds(pl.multiple_of(64 * z, 64), 64), 512:640] = part_q
    for d in range(3):
        arrived(tl.at[(ly + 3 - d) % 4], t_l[d])
    mean_diag = jnp.sum((tl[0] + tl[1]) + (tl[2] + tl[3])) / 512.0
    damping = damp_ratio * mean_diag
    ring = {}
    for s in range(1, 5):
        for kind, q in (("r", 0), ("l", 1), ("r", 1), ("l", 0)):
            if s < 4 or (kind, q) in (("r", 0), ("l", 1)):
                ring[(kind, s, q)] = (take(), take())
    right = {"dp": at((z + 1) % 8, x, h, c)}
    left = {"dp": at((z + 7) % 8, x, h, c)}

    def rows_at(cc, zz, q):
        return kin.at[pl.ds(pl.multiple_of(64 * zz + 32 * cc + 16 * q, 16), 16)]

    def pass_rows(kind, s, q):
        ref = rows_at(c, place(kind, s - 1), q)
        send(ref, ref, ring[(kind, s, q)][0], right if kind == "r" else left)

    swing = 2 * (z % 2) - 1
    home = z // 2
    order = [home, (home + 4 + swing) % 4, (home + 4 - swing) % 4, (home + 2) % 4]
    spans = [pl.ds(pl.multiple_of(128 * i, 128), 128) for i in order]
    shift = jnp.where(iota((128, 128), 0) == iota((128, 128), 1), damping, 0.0)
    spans.append(pl.ds(512, 128))

    def exact(u, v):
        return jnp.dot(u, v, precision=HIGH, preferred_element_type=F32)

    def eliminate(t):
        for m in range(5):
            a[t, m] = kin[spans[t], spans[m]] + shift if m == t else kin[spans[t], spans[m]]
        for n in range(t):
            for m in range(n + 1, 5):
                a[t, m] = a[t, m] - exact(a[t, n], a[n, m])
        inv = invert(a[t, t], lambda: take_hop(t + 2))
        for m in range(t + 1, 5):
            a[t, m] = exact(inv, a[t, m])

    for kind, q in (("r", 0), ("l", 1), ("r", 1), ("l", 0)):
        pass_rows(kind, 1, q)
    def take_hop(s):
        for kind, _, q in [n for n in ring if n[1] == s]:
            ref = rows_at(c, place(kind, s), q)
            arrived(ref, ring[(kind, s, q)][0])
            if (kind, s + 1, q) in ring:
                pass_rows(kind, s + 1, q)
            send(ref, ref, ring[(kind, s, q)][1], other)

    take_hop(1)
    for s in range(1, 5):
        for kind, _, q in [n for n in ring if n[1] == s]:
            arrived(rows_at(1 - c, place(kind, s), q), ring[(kind, s, q)][1])
        eliminate(s - 1)

    x3 = a[3, 4]
    x2 = a[2, 4] - exact(a[2, 3], x3)
    x1 = a[1, 4] - exact(a[1, 3], x3) - exact(a[1, 2], x2)
    pick = jnp.where(iota((8, 128), 1) == (me * 4 - 128 * home) + iota((8, 128), 0), 1.0, 0.0).astype(F32)
    own_x = exact(pick, a[0, 4])
    for n, value in ((3, x3), (2, x2), (1, x1)):
        own_x = own_x - exact(exact(pick, a[0, n]), value)
    own_x = own_x[0:4]
    lanes = iota((4, 128), 1)
    spot = iota((4, 8), 1)
    out = jnp.zeros((4, 8), F32)
    for n in range(8):
        chosen = jnp.sum(jnp.where(lanes == qidx[:, n : n + 1], own_x, 0.0), axis=1, keepdims=True)
        out = jnp.where(spot == n, chosen, out)
    scores[...] = jnp.sqrt(mean_diag) * out
    for copy in sent:
        copy.wait_send()


def run_front(act, grd, inb, outb, qry, lens, qidx):
    vmem = pl.BlockSpec(memory_space=pltpu.VMEM)
    hbm = pl.BlockSpec(memory_space=pltpu.HBM)
    return pl.pallas_call(
        front,
        out_shape=(jax.ShapeDtypeStruct((4, 4096), BF16), jax.ShapeDtypeStruct((4, 8), F32)),
        in_specs=[hbm] * 7,
        out_specs=(vmem, vmem),
        scratch_shapes=[
            pltpu.VMEM((512, 640), F32),
            pltpu.VMEM((4, 5, 128, 128), F32),
            pltpu.VMEM((8, 8, 128), F32),
            pltpu.VMEM((4, 8, 128), F32),
            pltpu.VMEM((4, 8), jnp.int32),
            pltpu.VMEM(act.shape, BF16),
            pltpu.VMEM(grd.shape, BF16),
            pltpu.VMEM(inb.shape, BF16),
            pltpu.VMEM(outb.shape, BF16),
            pltpu.VMEM(qry.shape, BF16),
            pltpu.SMEM((1, 4), jnp.int32),
            pltpu.VMEM((2, 8, 4, 256, 256), BF16),
            pltpu.VMEM((8, 2, 4, 64, 128), BF16),
            pltpu.VMEM((4, 2, 8, 64, 128), BF16),
            pltpu.VMEM((2, 4, 2, 128, 128), BF16),
            pltpu.VMEM((9, 128, 128), BF16),
            pltpu.VMEM((2, 4, 16, 256), F32),
            pltpu.VMEM((2, 4, 2, 16, 256), F32),
            pltpu.VMEM((2048, 512), BF16),
            pltpu.VMEM((256, 64), F32),
            pltpu.SemaphoreType.DMA((7,)),
            pltpu.SemaphoreType.DMA((SEMS,)),
            pltpu.SemaphoreType.DMA((SEMS,)),
        ],
        compiler_params=pltpu.CompilerParams(collective_id=0, has_side_effects=True, vmem_limit_bytes=48 * 1024 * 1024),
        name="front",
    )(*[pltpu.with_memory_space_constraint(v, pltpu.HBM) for v in (act, grd, inb, outb, qry, lens, qidx)])


def local(activations, out_grads, in_basis, out_basis, queries, pair_lengths, query_index):
    sketch, scores = run_front(
        activations[0], out_grads[0], in_basis[0].T, out_basis[0], queries[0], pair_lengths, query_index
    )
    return sketch[None], scores


def solution(mesh):
    placed = (
        P("layer", "dp", None),
        P("layer", "dp", None),
        P("layer", "dp", None),
        P("layer", "dp", None),
        P("layer", None, None),
        P("dp", None),
        P("dp", None),
    )
    return jax.shard_map(
        local,
        mesh=mesh,
        in_specs=placed,
        out_specs=(P("layer", "dp", None), P("dp", None)),
        check_vma=False,
    )
```

```python
import jax
import jax.numpy as jnp
from jax import lax
from jax.experimental import pallas as pl
from jax.experimental.pallas import tpu as pltpu
from jax.sharding import PartitionSpec as P

MESH = pl.DeviceIdType.MESH
damp_ratio = 0.5
F32 = jnp.float32
BF16 = jnp.bfloat16
NT = (((1,), (1,)), ((), ()))
SEMS = 192


def iota(shape, dim):
    return lax.broadcasted_iota(jnp.int32, shape, dim)


def onehot(cond):
    return jnp.where(cond, 1.0, 0.0).astype(BF16)


def pieces(v):
    hi = v.astype(BF16)
    rest = v - hi.astype(F32)
    mid = rest.astype(BF16)
    return hi, mid, (rest - mid.astype(F32)).astype(BF16)


def dot(a, b):
    return jnp.dot(a, b, preferred_element_type=F32)


def dot_nt(a, b):
    return lax.dot_general(a, b, NT, preferred_element_type=F32)


HIGH = lax.Precision.HIGHEST


STRIP = 64
PANEL = 16
PV = 2


def invert(d, between):
    sub = iota((8, 128), 0)
    lane = iota((8, 128), 1)
    big_row = iota((STRIP, 128), 0)
    big_col = iota((STRIP, 128), 1) // STRIP
    per = STRIP // 8
    count = 128 // STRIP
    strips = [d[STRIP * s : STRIP * s + STRIP, :] for s in range(count)]
    for s in range(count):
        rows = [strips[s][8 * i : 8 * i + 8, :] for i in range(per)]
        for p in range(0, per, PV):
            first = s * STRIP + 8 * p
            inside = lane // PANEL == first // PANEL
            heads = rows[p : p + PV]
            cols = [[jnp.broadcast_to(v[:, first + k : first + k + 1], (8, 128)) for v in heads] for k in range(PANEL)]
            heads = [
                jnp.where(inside, jnp.where(lane % PANEL == sub + 8 * n, 1.0, 0.0), v) for n, v in enumerate(heads)
            ]
            for k in range(PANEL):
                n0, r0 = k // 8, k % 8
                here = sub == r0
                f = cols[k]
                pivot = 1.0 / f[n0][r0 : r0 + 1, :]
                for j in range(k + 1, PANEL):
                    g = cols[j][n0][r0 : r0 + 1, :] * pivot
                    cols[j] = [
                        jnp.where(here, g, v - f[n] * g) if n == n0 else v - f[n] * g for n, v in enumerate(cols[j])
                    ]
                lead = heads[n0][r0 : r0 + 1, :] * pivot
                heads = [
                    jnp.where(here, lead, v - f[n] * lead) if n == n0 else v - f[n] * lead for n, v in enumerate(heads)
                ]
            rows[p : p + PV] = heads
            others = [i for i in range(per) if not p <= i < p + PV]
            if others:
                leads = [jnp.broadcast_to(heads[k // 8][k % 8 : k % 8 + 1, :], (8, 128)) for k in range(PANEL)]
                for i in others:
                    v = rows[i]
                    r = jnp.where(inside, 0.0, v)
                    for k in range(PANEL):
                        r = r - v[:, first + k : first + k + 1] * leads[k]
                    rows[i] = r
        done = jnp.concatenate(rows, axis=0) if per > 1 else rows[0]
        zero = jnp.zeros((STRIP, 128), F32)
        placed = jnp.concatenate([done if t == s else zero for t in range(count)], axis=0)
        new = [None] * count
        new[s] = done
        for t in [(s + i) % count for i in range(1, count)]:
            v = strips[t]
            side = jnp.where(big_col == s, v, 0.0)
            keep = jnp.where(big_col == s, 0.0, v)
            new[t] = keep - jnp.dot(side, placed, precision=HIGH, preferred_element_type=F32)
        strips = new
        if s == 0:
            between()
    return jnp.concatenate(strips, axis=0)


def front(act, grd, inb_hbm, outb_hbm, qry_hbm, lens_hbm, qidx_hbm, sk, scores, kin, a, tz, tl, qidx, av, gv, inb, outb, qry, lens, xs, wa, wb, srow, scol, lx, kb, perm, acc, in_sem, ssem, rsem):
    me = lax.axis_index("dp")
    ly = lax.axis_index("layer")
    c = me % 2
    h = (me // 2) % 2
    x = (me // 4) % 4
    z = me // 16
    b = me % 16

    def at(zz, xx, hh, cc):
        return ((zz * 4 + xx) * 2 + hh) * 2 + cc

    h_peer = at(z, x, 1 - h, c)
    c_peer = at(z, x, h, 1 - c)
    x_peers = [at(z, (x + d) % 4, h, c) for d in range(1, 4)]
    z_peers = [at((z + d) % 8, x, h, c) for d in range(1, 8)]

    load_a = pltpu.make_async_copy(act, av, in_sem.at[0])
    load_g = pltpu.make_async_copy(grd, gv, in_sem.at[1])
    load_l = pltpu.make_async_copy(lens_hbm, lens, in_sem.at[2])
    load_i = pltpu.make_async_copy(inb_hbm, inb, in_sem.at[3])
    load_o = pltpu.make_async_copy(outb_hbm, outb, in_sem.at[4])
    load_q = pltpu.make_async_copy(qry_hbm, qry, in_sem.at[5])
    load_x = pltpu.make_async_copy(qidx_hbm, qidx, in_sem.at[6])
    for load in (load_i, load_o, load_a, load_g, load_q, load_l, load_x):
        load.start()

    barrier = pltpu.get_barrier_semaphore()
    for peer in [h_peer, c_peer] + x_peers + z_peers:
        pl.semaphore_signal(barrier, inc=1, device_id={"dp": peer}, device_id_type=MESH)
    for d in range(1, 4):
        for hh in range(2):
            peer = {"dp": at(z, x, (h + hh) % 2, c), "layer": (ly + d) % 4}
            pl.semaphore_signal(barrier, inc=1, device_id=peer, device_id_type=MESH)

    used = [0]
    sent = []

    def take():
        used[0] += 1
        return used[0] - 1

    def send(src, dst, sem, device):
        copy = pltpu.make_async_remote_copy(
            src_ref=src, dst_ref=dst, send_sem=ssem.at[sem], recv_sem=rsem.at[sem], device_id=device, device_id_type=MESH
        )
        copy.start()
        sent.append(copy)

    def arrived(slot, sem):
        pltpu.make_async_remote_copy(
            src_ref=slot, dst_ref=slot, send_sem=ssem.at[sem], recv_sem=rsem.at[sem], device_id={"dp": c_peer}, device_id_type=MESH
        ).wait_recv()

    eye = onehot(iota((64, 64), 0) == iota((64, 64), 1))
    load_i.wait()
    load_o.wait()
    out_t = dot_nt(eye, outb[...]).astype(BF16)
    in_at = onehot(iota((76, 128), 0) == iota((76, 128), 1))
    out_at = onehot(iota((28, 128), 0) + 76 == iota((28, 128), 1))
    own = (dot(inb[...], in_at) + dot(out_t, out_at)).astype(BF16)

    @pl.when(c == 0)
    def _():
        wa[z, h, x] = own

    @pl.when(c == 1)
    def _():
        wb[x, h, z] = own

    def loaded():
        for load in (load_q, load_l, load_x, load_a, load_g):
            load.wait()

    def tables():
        q_row = iota((8, 64), 0)
        q_col = iota((8, 64), 1)
        low = onehot((q_row < 4) & (q_col == 4 * b + q_row))
        high = onehot((q_row >= 4) & (q_col == 4 * b + q_row - 4))
        tiles = [
            dot(low, qry[:, 256 * i : 256 * i + 128]) + dot(high, qry[:, 256 * i + 128 : 256 * i + 256]) for i in range(16)
        ]
        scol[8] = jnp.concatenate(tiles, axis=0).astype(BF16)
        lane = iota((128, 512), 0)
        col = iota((128, 512), 1)
        for j in range(16):
            perm[pl.ds(128 * j, 128), :] = onehot(col == ((lane // 4) % 8) * 64 + j * 4 + lane % 4)

    acc[...] = jnp.zeros_like(acc)

    sel_r = iota((256, 128), 0)
    sel_c = iota((256, 128), 1)

    def prepare(lo, hi):
        def body(part, carry):
            zl = part // 4
            xx = part % 4
            for hh in range(2):
                for cc in range(2):
                    i0 = zl * 16 + xx * 4 + hh * 2 + cc
                    ta = jnp.minimum((76 * i0) // 128, 17)
                    oa = 76 * i0 - 128 * ta
                    tg = jnp.minimum((28 * i0) // 128, 5)
                    og = 28 * i0 - 128 * tg
                    sel_a = onehot((sel_r == sel_c + oa) & (sel_c < 76))
                    sel_g = onehot((sel_r == sel_c - 76 + og) & (sel_c >= 76) & (sel_c < 104))
                    a4 = jnp.concatenate(
                        [av[:, pl.ds(pl.multiple_of((ta + 19 * n) * 128, 128), 256)] for n in range(4)], axis=0
                    )
                    g4 = jnp.concatenate(
                        [gv[:, pl.ds(pl.multiple_of((tg + 7 * n) * 128, 128), 256)] for n in range(4)], axis=0
                    )
                    xa = dot(a4, sel_a).astype(BF16)
                    xg = dot(g4, sel_g).astype(BF16)
                    for n in range(4):
                        xs[cc, 2 * n + zl, xx, 0:128, 128 * hh : 128 * hh + 128] = xa[128 * n : 128 * n + 128]
                        xs[cc, 2 * n + zl, xx, 128:256, 128 * hh : 128 * hh + 128] = xg[128 * n : 128 * n + 128]
            return carry

        lax.fori_loop(lo, hi, body, 0)

    def multiply_a(zz):
        for i in range(4):
            w = jnp.concatenate([wa[zz, 0, i], wa[zz, 1, i]], axis=1)
            acc[...] += dot_nt(xs[0, zz, i], w)

    def multiply_b(xx):
        def body(i, carry):
            for zz in (2 * i, 2 * i + 1):
                w = jnp.concatenate([wb[xx, 0, zz], wb[xx, 1, zz]], axis=1)
                acc[...] += dot_nt(xs[1, zz, xx], w)
            return carry

        lax.fori_loop(0, 4, body, 0)

    pl.semaphore_wait(barrier, 18)
    hand_a = {("r", 0, 0): take(), ("r", 0, 1): take()}
    pass_a = {}
    for s in range(1, 5):
        for kind, q in (("r", 0), ("l", 0), ("r", 1), ("l", 1)):
            if s < 4 or (kind, q) in (("r", 0), ("l", 1)):
                hand_a[(kind, s, q)] = take()
                pass_a[(kind, s, q)] = take()
    hand_b = {(n, q): take() for n in ("own", "left", "right", "far") for q in range(2)}
    pass_b = {n: take() for n in ("r0", "r1", "l0", "l1", "far0", "far1")}
    first = [take() for _ in range(15)]

    def place(kind, s):
        return (z + 8 - s) % 8 if kind == "r" else (z + s) % 8

    def slot_a(zz, q):
        return wa.at[zz, (h + q) % 2]

    far = (x + 2) % 4
    place_b = {"own": x, "left": (x + 3) % 4, "right": (x + 1) % 4, "far": far}
    other = {"dp": c_peer}

    @pl.when(c == 0)
    def _():
        base = len(sent)
        ref = wa.at[z, h, x]
        for i, peer in enumerate([h_peer] + x_peers):
            send(ref, ref, first[i], {"dp": peer})
        loaded()
        right = {"dp": at((z + 1) % 8, x, h, c)}
        left = {"dp": at((z + 7) % 8, x, h, c)}

        def pass_on(kind, s, q):
            ref = slot_a(place(kind, s - 1), q)
            send(ref, ref, pass_a[(kind, s, q)], right if kind == "r" else left)

        def hand(kind, s, q):
            ref = slot_a(place(kind, s), q)
            send(ref, ref, hand_a[(kind, s, q)], other)

        def hop(s, q):
            for kind in ("r", "l"):
                if (kind, s, q) in pass_a:
                    arrived(slot_a(place(kind, s), q), pass_a[(kind, s, q)])
                    if (kind, s + 1, q) in pass_a:
                        pass_on(kind, s + 1, q)
                    hand(kind, s, q)

        def theirs(name):
            for q in range(2):
                arrived(wb.at[place_b[name], (h + q) % 2], hand_b[(name, q)])
            multiply_b(place_b[name])

        for d in range(3):
            ref = wa.at[z, h, (x + 3 - d) % 4]
            arrived(ref, first[1 + d])
            send(ref, ref, first[4 + d], {"dp": h_peer})
        pass_on("r", 1, 0)
        pass_on("l", 1, 0)
        hand("r", 0, 0)
        prepare(0, 3)
        hop(1, 0)
        arrived(wa.at[z, 1 - h, x], first[0])
        for d in range(3):
            arrived(wa.at[z, 1 - h, (x + 3 - d) % 4], first[4 + d])
        pass_on("r", 1, 1)
        pass_on("l", 1, 1)
        hand("r", 0, 1)
        prepare(3, 5)
        hop(2, 0)
        prepare(5, 7)
        hop(1, 1)
        prepare(7, 8)
        hop(3, 0)
        multiply_a(z)
        hop(2, 1)
        multiply_a(place("r", 1))
        multiply_a(place("l", 1))
        theirs("own")
        hop(4, 0)
        hop(3, 1)
        multiply_a(place("r", 2))
        multiply_a(place("l", 2))
        theirs("left")
        theirs("right")
        hop(4, 1)
        multiply_a(place("r", 3))
        multiply_a(place("l", 3))
        theirs("far")
        multiply_a(place("r", 4))
        for copy in sent[base:]:
            copy.wait_send()
        del sent[base:]

    @pl.when(c == 1)
    def _():
        base = len(sent)
        ref = wb.at[x, h, z]
        for i, peer in enumerate([h_peer] + z_peers):
            send(ref, ref, first[i], {"dp": peer})
        loaded()
        for d in (0, 6, 1, 5, 2, 4, 3):
            ref = wb.at[x, h, (z + 7 - d) % 8]
            arrived(ref, first[1 + d])
            send(ref, ref, first[8 + d], {"dp": h_peer})
        right = {"dp": x_peers[0]}
        left = {"dp": x_peers[2]}
        xl, xr = place_b["left"], place_b["right"]

        def slot_b(xx, q):
            return wb.at[xx, (h + q) % 2]

        def spread_own(q):
            send(slot_b(x, q), slot_b(x, q), pass_b["r" + str(q)], right)
            send(slot_b(x, q), slot_b(x, q), pass_b["l" + str(q)], left)
            send(slot_b(x, q), slot_b(x, q), hand_b[("own", q)], other)

        def got_b(xx, q, name, to, sem, target):
            arrived(slot_b(xx, q), pass_b[name])
            if target is not None:
                send(slot_b(xx, q), slot_b(xx, q), pass_b[sem], target)
            send(slot_b(xx, q), slot_b(xx, q), hand_b[(to, q)], other)

        spread_own(0)
        prepare(0, 2)
        got_b(xl, 0, "r0", "left", "far0", right)
        got_b(xr, 0, "l0", "right", None, None)
        prepare(2, 3)
        arrived(wb.at[x, 1 - h, z], first[0])
        for d in range(7):
            arrived(wb.at[x, 1 - h, (z + 7 - d) % 8], first[8 + d])
        spread_own(1)
        got_b(far, 0, "far0", "far", None, None)
        prepare(3, 8)
        got_b(xr, 1, "l1", "right", "far1", left)
        got_b(xl, 1, "r1", "left", None, None)
        multiply_b(x)
        multiply_b(xl)
        multiply_b(xr)
        got_b(far, 1, "far1", "far", None, None)
        multiply_b(far)
        for s in range(5):
            for kind, q in (("r", 0), ("l", 0), ("r", 1), ("l", 1)):
                if (kind, s, q) in hand_a:
                    arrived(slot_a(place(kind, s), q), hand_a[(kind, s, q)])
            multiply_a(place("r", s))
            if 0 < s < 4:
                multiply_a(place("l", s))
        for copy in sent[base:]:
            copy.wait_send()
        del sent[base:]

    tok = iota((128, 64), 0)
    length = jnp.zeros((128, 64), jnp.int32)
    for p in range(4):
        length = jnp.where(tok // 32 == p, lens[0, p], length)
    mask = jnp.where(tok % 32 < length, 1.0, 0.0).astype(F32)
    right_proj = acc[0:128].astype(BF16)
    left_proj = (mask * acc[128:256]).astype(BF16)
    row = iota((128, 128), 0)
    colm = iota((128, 128), 1)
    mine = jnp.where(colm // 32 == row % 4, 1.0, 0.0).astype(F32)
    k_row = iota((128, 64), 0)
    k_col = iota((128, 64), 1)
    j_row = iota((64, 128), 0)
    j_col = iota((64, 128), 1)
    total = jnp.zeros((128, 128), F32)
    for par in range(2):
        spread = dot_nt(onehot(k_col == 2 * (k_row // 4) + par), left_proj)
        lefts = (spread * mine).astype(BF16)
        rights = dot(right_proj, onehot(j_col == j_row + 64 * par)).astype(BF16)
        total = total + dot(lefts, rights)
    sketch = total.astype(BF16)
    for m in range(32):
        sk[:, 128 * m : 128 * m + 128] = total[4 * m : 4 * m + 4].astype(BF16)
    srow[c, x, h] = sketch
    scol[z] = sketch

    s_h = take()
    send(srow.at[c, x, h], srow.at[c, x, h], s_h, {"dp": h_peer})
    s_z = [take() for _ in range(7)]
    for d in range(7):
        send(scol.at[z], scol.at[z], s_z[d], {"dp": z_peers[d]})
    tables()
    arrived(srow.at[c, x, 1 - h], s_h)
    s_x = [take() for _ in range(3)]
    s_c = [take() for _ in range(4)]
    for d in range(3):
        send(srow.at[c, x], srow.at[c, x], s_x[d], {"dp": x_peers[d]})
    send(srow.at[c, x], srow.at[c, x], s_c[0], {"dp": c_peer})
    for d in range(3):
        xx = (x + 3 - d) % 4
        arrived(srow.at[c, xx], s_x[d])
        send(srow.at[c, xx], srow.at[c, xx], s_c[d + 1], {"dp": c_peer})
    for d in range(7):
        arrived(scol.at[(z + 7 - d) % 8], s_z[d])
    for d in range(4):
        arrived(srow.at[1 - c, (x + 4 - d) % 4], s_c[d])

    squares = jnp.zeros((8, 128), F32)
    for cc in range(2):
        for xx in range(4):
            v = srow[cc, xx].astype(F32)
            squares = squares + jnp.sum((v * v).reshape(32, 8, 128), axis=0)
    tz[z] = squares
    t_z = [take() for _ in range(7)]
    for d in range(7):
        send(tz.at[z], tz.at[z], t_z[d], {"dp": z_peers[d]})
    gram = jnp.zeros((256, 144), F32)
    for u in range(4):
        rows = [srow[:, :, :, pl.ds(32 * u + 16 * v, 16), :].reshape(256, 128) for v in range(2)]
        cols = [scol[:, pl.ds(32 * u + 16 * v, 16), :].reshape(144, 128) for v in range(2)]
        gram = gram + dot_nt(jnp.concatenate(rows, axis=1), jnp.concatenate(cols, axis=1))
    gr = iota((256, 144), 0)
    gc = iota((256, 144), 1)
    gram = jnp.where((gr // 4) % 4 == (gc // 4) % 4, gram, 0.0)
    pr = iota((64, 256), 0)
    pc = iota((64, 256), 1)
    blk = pc // 16
    pick_rows = onehot(pr == ((blk // 2) % 4) * 16 + (blk % 2) * 8 + (blk // 8) * 4 + pc % 4)
    half = sum(dot(pick_rows, v) for v in pieces(gram))
    nr = iota((144, 256), 0)
    nc = iota((144, 256), 1)
    in_k = (nr < 128) & (nc < 128) & (nc % 32 == (nr // 16) * 4 + nr % 4)
    in_q = (nr >= 128) & (nc >= 128) & ((nc - 128) // 16 == b % 8) & (nc % 4 == nr % 4)
    pick_cols = onehot(in_k | in_q)
    spread = sum(dot(v, pick_cols) for v in pieces(half))
    yr = iota((64, 256), 0)
    yc = iota((64, 256), 1)
    quarter = jnp.where(yc < 128, yc // 32, (yc // 4) % 4) == yr // 16
    spread = jnp.where(quarter, spread, 0.0)
    lx[h, ly] = spread[0:16] + spread[16:32] + spread[32:48] + spread[48:64]

    l_s = [(d, hh, take()) for d in range(4) for hh in range(2) if d + hh > 0]
    for d, hh, sem in l_s:
        peer = {"dp": at(z, x, (h + hh) % 2, c), "layer": (ly + d) % 4}
        send(lx.at[h, ly], lx.at[h, ly], sem, peer)
    for d, hh, sem in l_s:
        arrived(lx.at[(h + hh) % 2, (ly + 4 - d) % 4], sem)
    for hh in range(2):
        kb[c, x, hh] = (lx[hh, 0] + lx[hh, 1]) + (lx[hh, 2] + lx[hh, 3])
    for d in range(7):
        arrived(tz.at[(z + 7 - d) % 8], t_z[d])
    plane_sums = tz[0]
    for n in range(1, 8):
        plane_sums = plane_sums + tz[n]
    tl[ly] = plane_sums
    t_l = [take() for _ in range(3)]
    for d in range(3):
        send(tl.at[ly], tl.at[ly], t_l[d], {"layer": (ly + 1 + d) % 4})
    k_x = [take() for _ in range(3)]
    k_c = [take() for _ in range(4)]
    for d in range(3):
        send(kb.at[c, x], kb.at[c, x], k_x[d], {"dp": x_peers[d]})
    send(kb.at[c, x], kb.at[c, x], k_c[0], {"dp": c_peer})
    for d in range(3):
        xx = (x + 3 - d) % 4
        arrived(kb.at[c, xx], k_x[d])
        send(kb.at[c, xx], kb.at[c, xx], k_c[d + 1], {"dp": c_peer})
    for d in range(4):
        arrived(kb.at[1 - c, (x + 4 - d) % 4], k_c[d])

    def tall(v):
        return jnp.concatenate([v, v, v, v], axis=0)

    r4 = iota((64, 128), 0) // 16
    l4 = iota((64, 128), 1)
    wide = []
    side = [jnp.zeros((16, 128), F32), jnp.zeros((16, 128), F32)]
    for j in range(16):
        v = kb[j % 2, j // 4, (j // 2) % 2]
        wide.append(jnp.where(l4 // 32 == r4, tall(v[:, 0:128]), 0.0))
        side[j // 8] = side[j // 8] + v[:, 128:256]
    flat = jnp.concatenate(wide, axis=1)
    part = sum(dot(v, perm[...]) for v in pieces(flat))
    sides = jnp.concatenate([jnp.where((l4 // 4) % 4 == r4, tall(v), 0.0) for v in side], axis=1)
    ir = iota((256, 128), 0)
    ic = iota((256, 128), 1)
    place_q = onehot(ic == (ir // 16) * 4 + ir % 4)
    part_q = sum(dot(v, place_q) for v in pieces(sides))
    kin[pl.ds(pl.multiple_of(64 * z, 64), 64), 0:512] = part
    kin[pl.ds(pl.multiple_of(64 * z, 64), 64), 512:640] = part_q
    for d in range(3):
        arrived(tl.at[(ly + 3 - d) % 4], t_l[d])
    mean_diag = jnp.sum((tl[0] + tl[1]) + (tl[2] + tl[3])) / 512.0
    damping = damp_ratio * mean_diag
    ring = {}
    for s in range(1, 5):
        for kind, q in (("r", 0), ("l", 1), ("r", 1), ("l", 0)):
            if s < 4 or (kind, q) in (("r", 0), ("l", 1)):
                ring[(kind, s, q)] = (take(), take())
    right = {"dp": at((z + 1) % 8, x, h, c)}
    left = {"dp": at((z + 7) % 8, x, h, c)}

    def rows_at(cc, zz, q):
        return kin.at[pl.ds(pl.multiple_of(64 * zz + 32 * cc + 16 * q, 16), 16)]

    def pass_rows(kind, s, q):
        ref = rows_at(c, place(kind, s - 1), q)
        send(ref, ref, ring[(kind, s, q)][0], right if kind == "r" else left)

    swing = 2 * (z % 2) - 1
    home = z // 2
    order = [home, (home + 4 + swing) % 4, (home + 4 - swing) % 4, (home + 2) % 4]
    spans = [pl.ds(pl.multiple_of(128 * i, 128), 128) for i in order]
    shift = jnp.where(iota((128, 128), 0) == iota((128, 128), 1), damping, 0.0)
    spans.append(pl.ds(512, 128))

    def exact(u, v):
        return jnp.dot(u, v, precision=HIGH, preferred_element_type=F32)

    def eliminate(t):
        for m in range(5):
            a[t, m] = kin[spans[t], spans[m]] + shift if m == t else kin[spans[t], spans[m]]
        for n in range(t):
            for m in range(n + 1, 5):
                a[t, m] = a[t, m] - exact(a[t, n], a[n, m])
        inv = invert(a[t, t], lambda: take_hop(t + 2))
        for m in range(t + 1, 5):
            a[t, m] = exact(inv, a[t, m])

    for kind, q in (("r", 0), ("l", 1), ("r", 1), ("l", 0)):
        pass_rows(kind, 1, q)
    def take_hop(s):
        for kind, _, q in [n for n in ring if n[1] == s]:
            ref = rows_at(c, place(kind, s), q)
            arrived(ref, ring[(kind, s, q)][0])
            if (kind, s + 1, q) in ring:
                pass_rows(kind, s + 1, q)
            send(ref, ref, ring[(kind, s, q)][1], other)

    take_hop(1)
    for s in range(1, 5):
        for kind, _, q in [n for n in ring if n[1] == s]:
            arrived(rows_at(1 - c, place(kind, s), q), ring[(kind, s, q)][1])
        eliminate(s - 1)

    x3 = a[3, 4]
    x2 = a[2, 4] - exact(a[2, 3], x3)
    x1 = a[1, 4] - exact(a[1, 3], x3) - exact(a[1, 2], x2)
    pick = jnp.where(iota((8, 128), 1) == (me * 4 - 128 * home) + iota((8, 128), 0), 1.0, 0.0).astype(F32)
    own_x = exact(pick, a[0, 4])
    for n, value in ((3, x3), (2, x2), (1, x1)):
        own_x = own_x - exact(exact(pick, a[0, n]), value)
    own_x = own_x[0:4]
    lanes = iota((4, 128), 1)
    spot = iota((4, 8), 1)
    out = jnp.zeros((4, 8), F32)
    for n in range(8):
        chosen = jnp.sum(jnp.where(lanes == qidx[:, n : n + 1], own_x, 0.0), axis=1, keepdims=True)
        out = jnp.where(spot == n, chosen, out)
    scores[...] = jnp.sqrt(mean_diag) * out
    for copy in sent:
        copy.wait_send()


def run_front(act, grd, inb, outb, qry, lens, qidx):
    vmem = pl.BlockSpec(memory_space=pltpu.VMEM)
    hbm = pl.BlockSpec(memory_space=pltpu.HBM)
    return pl.pallas_call(
        front,
        out_shape=(jax.ShapeDtypeStruct((4, 4096), BF16), jax.ShapeDtypeStruct((4, 8), F32)),
        in_specs=[hbm] * 7,
        out_specs=(vmem, vmem),
        scratch_shapes=[
            pltpu.VMEM((512, 640), F32),
            pltpu.VMEM((4, 5, 128, 128), F32),
            pltpu.VMEM((8, 8, 128), F32),
            pltpu.VMEM((4, 8, 128), F32),
            pltpu.VMEM((4, 8), jnp.int32),
            pltpu.VMEM(act.shape, BF16),
            pltpu.VMEM(grd.shape, BF16),
            pltpu.VMEM(inb.shape, BF16),
            pltpu.VMEM(outb.shape, BF16),
            pltpu.VMEM(qry.shape, BF16),
            pltpu.SMEM((1, 4), jnp.int32),
            pltpu.VMEM((2, 8, 4, 256, 256), BF16),
            pltpu.VMEM((8, 2, 4, 64, 128), BF16),
            pltpu.VMEM((4, 2, 8, 64, 128), BF16),
            pltpu.VMEM((2, 4, 2, 128, 128), BF16),
            pltpu.VMEM((9, 128, 128), BF16),
            pltpu.VMEM((2, 4, 16, 256), F32),
            pltpu.VMEM((2, 4, 2, 16, 256), F32),
            pltpu.VMEM((2048, 512), BF16),
            pltpu.VMEM((256, 64), F32),
            pltpu.SemaphoreType.DMA((7,)),
            pltpu.SemaphoreType.DMA((SEMS,)),
            pltpu.SemaphoreType.DMA((SEMS,)),
        ],
        compiler_params=pltpu.CompilerParams(collective_id=0, has_side_effects=True, vmem_limit_bytes=48 * 1024 * 1024),
        name="front",
    )(*[pltpu.with_memory_space_constraint(v, pltpu.HBM) for v in (act, grd, inb, outb, qry, lens, qidx)])


def local(activations, out_grads, in_basis, out_basis, queries, pair_lengths, query_index):
    sketch, scores = run_front(
        activations[0], out_grads[0], in_basis[0].T, out_basis[0], queries[0], pair_lengths, query_index
    )
    return sketch[None], scores


def solution(mesh):
    placed = (
        P("layer", "dp", None),
        P("layer", "dp", None),
        P("layer", "dp", None),
        P("layer", "dp", None),
        P("layer", None, None),
        P("dp", None),
        P("dp", None),
    )
    return jax.shard_map(
        local,
        mesh=mesh,
        in_specs=placed,
        out_specs=(P("layer", "dp", None), P("dp", None)),
        check_vma=False,
    )
```
